256 devices in a mesh: member: 8 (over x, core), tx: 4 (over y), ty: 8 (over z).
Axes of the slice: x: 4, y: 4, z: 8, core: 2. Of those that a mesh axis runs over, the one named last changes fastest.
Arguments:
- state: float32 [4096, 256, 128], P(('member', 'tx'), 'ty'), parts along dimension 0, may hold values from -6 to 6
- courant: bfloat16 [4096, 256, 128], P(('member', 'tx'), 'ty'), parts along dimension 0, may hold values from -0.3984375 to 0.3984375
- diffusion: float32 [4096, 256], P(('member', 'tx'), 'ty'), parts along dimension 0, may hold values from 0.02 to 0.2
- conv_mask: int32 [4096, 256], P(('member', 'tx'), 'ty'), parts along dimension 0, may hold values from 0 to 1, as said below
- w_in: bfloat16 [128, 1024], replicated, may hold values from -0.5 to 0.5
- w_hidden: bfloat16 [3, 1024, 1024], replicated, may hold values from -0.1875 to 0.1875
- w_out: bfloat16 [1024, 128], replicated, may hold values from -0.1875 to 0.1875
Outputs:
- state_out: float32 [4096, 256, 128], P(('member', 'tx'), 'ty'), parts along dimension 0
The draws below stay inside these ranges and needn't reach their ends.
There are 8 independent parts, one for each index of `member`. The reference program is written for one: setup_inputs(seed, part) draws one part's arguments, and reference() takes and returns one part's arrays. A program takes and returns all parts, laid end to end along the dimension named above; an argument that names none is the same for every part. Nothing has to cross between parts.
Inputs may be any that keep to these rules, and one draw needn't show every extreme that they name: `conv_mask`: A tile is one device's 128 x 32 columns. A tile's used blocks are ceil(its flagged columns / 32); at most 64, reached by some tile; over a member's tiles they sum to exactly 1056.
All inputs are finite; a program needn't handle non-finite values.
Results may differ from the reference program's by a relative error of at most 0.00033.
Values may be sent and summed in bfloat16 or wider, within the bound.
No kernel may reach another device: no remote copies, remote signals or barrier semaphores. Data moves between devices by JAX's collectives and lax.ppermute only.
A program may use at most 64 MiB of HBM per device.

```python
import math
import jax
import jax.numpy as jnp
from jax import lax

CLON = 128
CLAT = 32
LEV = 64
CH = 128
HID = 1024
LAYERS = 5
BLK = 32
NBLK = 64
MEAN = 33
NLON = 512
NLAT = 256
N_TX = 4
N_TY = 8


def tile_order(sub_key):
    return jax.random.permutation(sub_key, CLON * CLAT)


def draw_conv_mask(key, part):
    tile_count = N_TX * N_TY
    half_count = tile_count // 2
    key_pair = jax.random.fold_in(key, 3)
    key_perm = jax.random.fold_in(key, 5)
    key_trim = jax.random.fold_in(key, 7)
    key_rank = jax.random.fold_in(key, 11)
    first = jax.random.randint(key_pair, (half_count,), 2, 2 * MEAN - 1)
    first = first.at[0].set(NBLK)
    loads = jnp.concatenate([first, 2 * MEAN - first])
    loads = jax.random.permutation(key_perm, loads)
    trimmed = jax.random.randint(key_trim, (tile_count,), 0, BLK)
    trimmed = jnp.where(loads == NBLK, 0, trimmed)
    flagged = loads * BLK - trimmed
    ranks = jax.vmap(tile_order)(jax.random.split(key_rank, tile_count))
    marks = (ranks < flagged[:, None]).astype(jnp.int32)
    marks = marks.reshape(N_TX, N_TY, CLON, CLAT).transpose(0, 2, 1, 3)
    return marks.reshape(N_TX * CLON, N_TY * CLAT)


def block_scale(stream_key, extent, shards, least, largest):
    def one(position, shards_of):
        steps = jax.random.uniform(jax.random.fold_in(jax.random.fold_in(stream_key, 6), position), (shards_of,), jnp.float32, least / len(shards), largest / len(shards))
        return jnp.repeat(jnp.exp(steps), extent[position] // shards_of).reshape((-1,) + (1,) * (len(extent) - position - 1))

    loudness = one(*shards[0])
    for cut in shards[1:]:
        loudness = loudness * one(*cut)
    return loudness


def noise(own_key, shape, width, most, pieces=(), kind=jnp.bfloat16):
    result = jax.random.normal(own_key, shape, jnp.float32) * width
    if len(pieces) > 0:
        result = block_scale(own_key, shape, pieces, -0.22, 0.18) * result
    return jnp.clip(result, min=-most, max=most).astype(kind)


def setup_inputs(seed: int = 0, part: int = 0) -> dict:
    key_of = jax.random.split(jax.random.key(seed), 8)
    part_splits = jax.random.split(jax.random.fold_in(key_of[7], part), 8)
    return {
        "state": noise(part_splits[0], (NLON, NLAT, CH), 1.0, 6.0, ((0, 4), (1, 8)), jnp.float32),
        "courant": jnp.clip(jax.random.uniform(part_splits[1], (NLON, NLAT, CH), jnp.float32, -0.3984375, 0.3984375) * block_scale(part_splits[1], (NLON, NLAT, CH), ((0, 4), (1, 8)), -0.4, 0.0), -0.3984375, 0.3984375).astype(jnp.bfloat16),
        "diffusion": jnp.clip(jnp.exp(math.log(0.2) - 2.3025851 * jax.random.uniform(part_splits[2], (NLON, NLAT), jnp.float32) ** block_scale(part_splits[2], (NLON, NLAT), ((0, 4), (1, 8)), -0.2, 0.2)), 0.02, 0.2),
        "conv_mask": draw_conv_mask(jax.random.fold_in(jax.random.fold_in(key_of[7], part), 71), part),
        "w_in": noise(key_of[4], (CH, HID), CH ** -0.5, 0.5),
        "w_hidden": noise(key_of[5], (LAYERS - 2, HID, HID), HID ** -0.5, 0.1875),
        "w_out": noise(key_of[6], (HID, CH), HID ** -0.5, 0.1875),
    }


def advance(state, courant, diffusion):
    east = jnp.roll(state, -1, 0)
    west = jnp.roll(state, 1, 0)
    zero_line = jnp.zeros_like(state[:, :1])
    north = jnp.concatenate([state[:, 1:], zero_line], 1)
    south = jnp.concatenate([zero_line, state[:, :-1]], 1)
    wind = courant.astype(jnp.float32)
    along_lon = jnp.concatenate([wind[..., :LEV], wind[..., :LEV]], -1)
    along_lat = jnp.concatenate([wind[..., LEV:], wind[..., LEV:]], -1)
    laplace = east + west + north + south - 4.0 * state
    return state - 0.5 * along_lon * (east - west) - 0.5 * along_lat * (north - south) + diffusion[..., None] * laplace


def closure(inputs, w_in, w_hidden, w_out):
    hidden = jax.nn.silu(jnp.dot(inputs, w_in, preferred_element_type=jnp.float32)).astype(jnp.bfloat16)
    for layer_idx in range(w_hidden.shape[0]):
        hidden = jax.nn.silu(jnp.dot(hidden, w_hidden[layer_idx], preferred_element_type=jnp.float32)).astype(jnp.bfloat16)
    return jnp.dot(hidden, w_out, preferred_element_type=jnp.float32).astype(jnp.bfloat16)


def reference(state, courant, diffusion, conv_mask, w_in, w_hidden, w_out):
    advanced = advance(state, courant, diffusion)
    columns = NLON * NLAT
    capacity = N_TX * N_TY * MEAN * BLK
    flags = conv_mask.reshape(columns).astype(jnp.int32)
    ranks = (jnp.cumsum(flags) - 1).astype(jnp.int32)
    slot_pos = jnp.where(flags == 1, ranks, capacity).astype(jnp.int32)
    features = advanced.reshape(columns, CH).astype(jnp.bfloat16)
    packed = jnp.zeros((capacity, CH), jnp.bfloat16).at[slot_pos].set(features, mode="drop")
    groups = packed.reshape(N_TX * N_TY, MEAN * BLK, CH)
    tendency = lax.map(lambda group: closure(group, w_in, w_hidden, w_out), groups)
    tendency = tendency.reshape(capacity, CH)
    picked = tendency[jnp.minimum(slot_pos, capacity - 1)].astype(jnp.float32)
    added = jnp.where(flags[:, None] == 1, picked, jnp.float32(0.0))
    return (advanced.reshape(columns, CH) + added).reshape(NLON, NLAT, CH)
```

```python
import functools

import jax
import jax.numpy as jnp
from jax import lax
from jax.experimental import pallas as pl
from jax.experimental.pallas import tpu as pltpu
from jax.sharding import PartitionSpec as P

LON, LAT, CH, HID = 128, 32, 128, 1024
COLS = LON * LAT
TILE = 512
CAP = 2048
ROWS = CAP + TILE
PGRP = 256
UGRP = 128
EDGE = 384
BF, F32, I32 = jnp.bfloat16, jnp.float32, jnp.int32


def iota(shape, dim):
    return lax.broadcasted_iota(I32, shape, dim)


def one_hot(hit):
    return jnp.where(hit, F32(1.0), F32(0.0)).astype(BF)


def mm(a, b):
    return jnp.dot(a, b, preferred_element_type=F32)


def silu(v):
    half = 0.5 * v
    return (half + half * jnp.tanh(half)).astype(BF)


def closure_tile(x, w_in, w_hid, w_out, ha, hb):
    step = 256

    def layer(src, weight, dst):
        for n in range(0, HID, step):
            dst[:, n : n + step] = silu(mm(src, weight(n)))

    layer(x, lambda n: w_in[:, n : n + step], ha)
    layer(ha[...], lambda n: w_hid[0, :, n : n + step], hb)
    layer(hb[...], lambda n: w_hid[1, :, n : n + step], ha)
    layer(ha[...], lambda n: w_hid[2, :, n : n + step], hb)
    return mm(hb[...], w_out[...]).astype(BF)


def append(packed, hits, features, aligned):
    rows = mm(one_hot(hits), features)
    n = rows.shape[0]
    head = packed[pl.ds(aligned, 16), :].astype(F32) + rows[:16]
    packed[pl.ds(aligned, 16), :] = head.astype(BF)
    packed[pl.ds(pl.multiple_of(aligned + 16, 16), n - 16), :] = rows[16:].astype(BF)


def align16(x):
    return pl.multiple_of((x // 16) * 16, 16)


def first_kernel(
    state_h, courant_h, diff_h, mask_h, win_h, whid_h, wout_h,
    adv, packed, tend, rank_t, rank_e, scal, coef, w_in, w_hid, w_out,
    st, cou, dif, msk, dif_t, rank_n, rank_r, tmp, ha, hb, scal_s, sem, sem_s,
):
    quarter = COLS // 4

    def in_copies(k):
        return (
            pltpu.make_async_copy(state_h.at[pl.ds(k * quarter, quarter)], st.at[pl.ds(k * quarter + LAT, quarter)], sem.at[k]),
            pltpu.make_async_copy(courant_h.at[pl.ds(k * quarter, quarter)], cou.at[pl.ds(k * quarter, quarter)], sem.at[4 + k]),
        )

    mask_copy = pltpu.make_async_copy(mask_h, msk, sem.at[8])
    diff_copy = pltpu.make_async_copy(diff_h, dif, sem.at[9])
    w_copies = (
        pltpu.make_async_copy(win_h, w_in, sem.at[10]),
        pltpu.make_async_copy(whid_h, w_hid, sem.at[11]),
        pltpu.make_async_copy(wout_h, w_out, sem.at[12]),
    )
    mask_copy.start()
    diff_copy.start()
    for k in range(4):
        for c in in_copies(k):
            c.start()
    for c in w_copies:
        c.start()
    packed[...] = jnp.zeros_like(packed)
    tend[...] = jnp.zeros_like(tend)
    st[0:LAT, :] = jnp.zeros((LAT, CH), F32)
    st[COLS + LAT : COLS + 2 * LAT, :] = jnp.zeros((LAT, CH), F32)

    mask_copy.wait()
    lon, lat = iota((LON, LAT), 0), iota((LON, LAT), 1)
    flags = msk[...]
    inner = (lon > 0) & (lon < LON - 1) & (lat > 0) & (lat < LAT - 1) & (flags == 1)
    inner_b = one_hot(inner)
    before = one_hot(iota((LAT, LAT), 0) < iota((LAT, LAT), 1))
    in_row = mm(inner_b, before)
    rows_below = one_hot(iota((LON, LON), 1) < iota((LON, LON), 0))
    per_lat = mm(rows_below, inner_b).astype(BF)
    row_start = mm(per_lat, jnp.ones((LAT, LON), BF))
    rank = jnp.where(inner, in_row + row_start[:, :LAT], F32(-4096.0))
    wide = jnp.concatenate([rank, jnp.zeros((LON, LON - LAT), F32)], axis=1)
    rank_n[...] = wide
    rank_t[...] = jnp.transpose(wide)[:LAT].astype(I32)
    rank_r[...] = jnp.concatenate(
        [rank_n[pl.ds(j, COLS // PGRP, stride=PGRP // LAT), :LAT] for j in range(PGRP // LAT)], axis=1
    ).astype(I32)
    starts = jnp.transpose(row_start)[:1]

    flags_f = flags.astype(F32)
    flags_w = jnp.concatenate([flags_f, jnp.zeros((LON, LON - LAT), F32)], axis=1)
    flags_t = jnp.transpose(flags_w)
    lane = iota((1, LON), 1)
    ends = (lane == 0) | (lane == LON - 1)
    edge_row = jnp.concatenate(
        [
            flags_f[:1],
            flags_f[LON - 1 :],
            jnp.zeros((1, 64), F32),
            jnp.where(ends, F32(0.0), flags_t[:1]),
            jnp.where(ends, F32(0.0), flags_t[LAT - 1 : LAT]),
        ],
        axis=1,
    )
    edge_b = jnp.broadcast_to(edge_row, (16, EDGE)).astype(BF)
    edge_before = one_hot(iota((EDGE, EDGE), 0) < iota((EDGE, EDGE), 1))
    edge_rank = mm(edge_b, edge_before)[:8]
    inner_n = starts[:, LON - 1 :]
    rank_e[...] = jnp.where(edge_row == 1.0, edge_rank + inner_n, F32(-4096.0)).astype(I32)
    edge_n = jnp.broadcast_to(jnp.sum(edge_row, axis=1, keepdims=True), (1, LON))
    rows8 = iota((8, LON), 0)
    scal[...] = jnp.where(rows8 == 0, starts, edge_n).astype(I32)
    scal_copy = pltpu.make_async_copy(scal, scal_s, sem_s)
    scal_copy.start()
    diff_copy.wait()
    dif_w = jnp.concatenate([dif[...], jnp.zeros((LON, LON - LAT), F32)], axis=1)
    dif_t[...] = jnp.transpose(dif_w)[:LAT]
    scal_copy.wait()

    for c in in_copies(0):
        c.wait()

    def group(g, carry):
        k = lax.div(g, 4)

        @pl.when((lax.rem(g, 4) == 3) & (g < 15))
        def _():
            for c in in_copies(k + 1):
                c.wait()

        r = pl.multiple_of(g * PGRP, PGRP)
        center = st[pl.ds(r + LAT, PGRP), :]
        east = st[pl.ds(r + 2 * LAT, PGRP), :]
        west = st[pl.ds(r, PGRP), :]
        row = iota((PGRP, CH), 0)
        lat_of = lax.rem(row, LAT)
        north = jnp.where(lat_of == LAT - 1, F32(0.0), st[pl.ds(r + LAT + 1, PGRP), :])
        south = jnp.where(lat_of == 0, F32(0.0), st[pl.ds(r + LAT - 1, PGRP), :])
        wind = 0.5 * cou[pl.ds(r, PGRP), :].astype(F32)
        turned = pltpu.roll(wind, 64, 1)
        low = iota((PGRP, CH), 1) < 64
        along_lon = jnp.where(low, wind, turned)
        along_lat = jnp.where(low, turned, wind)
        d8 = pltpu.roll(dif_t[...], lax.rem(LON - g * 8, LON), 1)
        d = jnp.concatenate([jnp.broadcast_to(d8[:, j : j + 1], (LAT, CH)) for j in range(8)], axis=0)
        laplace = east + west + north + south - 4.0 * center
        new = center - along_lon * (east - west) - along_lat * (north - south) + d * laplace
        adv[pl.ds(r, PGRP), :] = new
        tmp[...] = d - along_lat
        coef[pl.ds(pl.multiple_of(g * 8, 8), 8), :] = tmp[pl.ds(LAT - 1, 8, stride=LAT), :]
        tmp[...] = d + along_lat
        coef[pl.ds(pl.multiple_of(LON + g * 8, 8), 8), :] = tmp[pl.ds(0, 8, stride=LAT), :]

        @pl.when(g == 0)
        def _():
            coef[2 * LON : 2 * LON + LAT, :] = (d + along_lon)[:LAT]

        @pl.when(g == 15)
        def _():
            coef[2 * LON + LAT : 2 * LON + 2 * LAT, :] = (d - along_lon)[PGRP - LAT :]

        aligned = align16(scal_s[0, g * 8])
        hits = iota((PGRP + 16, PGRP), 0) == rank_r[pl.ds(g, 1), :] - aligned
        append(packed, hits, new.astype(BF), aligned)
        return carry

    lax.fori_loop(0, 16, group, 0)
    for c in w_copies:
        c.wait()

    @pl.when(scal_s[0, LON - 1] >= TILE)
    def _():
        tend[:TILE, :] = closure_tile(packed[:TILE, :], w_in, w_hid, w_out, ha, hb)


def second_kernel(
    west, east, south, north, adv_i, packed_i, tend_i, rank_t, rank_e, scal, coef, w_in, w_hid, w_out,
    out_h, adv, packed, tend, ha, hb, scal_s, sem_s, sem,
):
    scal_copy = pltpu.make_async_copy(scal, scal_s, sem_s)
    scal_copy.start()
    adv[...] = adv_i[...]
    packed[...] = packed_i[...]
    tend[...] = tend_i[...]
    adv[0:LAT, :] += west[...] * coef[2 * LON : 2 * LON + LAT, :]
    adv[COLS - LAT :, :] += east[...] * coef[2 * LON + LAT :, :]
    low, high = pl.ds(0, LON, stride=LAT), pl.ds(LAT - 1, LON, stride=LAT)
    adv[high, :] = adv[high, :] + north[...] * coef[:LON, :]
    adv[low, :] = adv[low, :] + south[...] * coef[LON : 2 * LON, :]
    edge = jnp.concatenate(
        [adv[0:LAT, :], adv[COLS - LAT :, :], jnp.zeros((64, CH), F32), adv[low, :], adv[high, :]], axis=0
    ).astype(BF)
    scal_copy.wait()
    inner_n = scal_s[0, LON - 1]
    count = inner_n + scal_s[1, 0]
    aligned_e = align16(inner_n)
    hits = iota((320 + 16, EDGE), 0) == rank_e[:1, :] - aligned_e
    append(packed, hits, edge, aligned_e)

    def tile(t, carry):
        r = pl.multiple_of(t * TILE, TILE)
        tend[pl.ds(r, TILE), :] = closure_tile(packed[pl.ds(r, TILE), :], w_in, w_hid, w_out, ha, hb)
        return carry

    done = jnp.where(inner_n >= TILE, 1, 0)
    lax.fori_loop(done, lax.div(count + TILE - 1, TILE), tile, 0)

    rank_col = jnp.concatenate(
        [jnp.transpose(jnp.broadcast_to(rank_e[:1, k * 128 : k * 128 + 128], (128, 128))) for k in range(3)], axis=0
    )
    picks = jnp.concatenate([rank_col - aligned_e - 128 * k for k in range(3)], axis=1) == lax.rem(
        iota((EDGE, EDGE), 1), 128
    )
    back = mm(one_hot(picks), tend[pl.ds(aligned_e, EDGE), :])
    adv[0:LAT, :] += back[0:LAT]
    adv[COLS - LAT :, :] += back[LAT : 2 * LAT]
    adv[low, :] = adv[low, :] + back[128:256]
    adv[high, :] = adv[high, :] + back[256:384]

    def out_copy(k):
        part = pl.ds(k * (COLS // 8), COLS // 8)
        return pltpu.make_async_copy(adv.at[part], out_h.at[part], sem.at[k])

    def unpack(g, carry):
        r = pl.multiple_of(g * UGRP, UGRP)
        aligned = align16(scal_s[0, g * 4])
        local = rank_t[...] - aligned
        local = pltpu.roll(local, lax.rem(LON - g * 4, LON), 1)
        col = jnp.concatenate([jnp.broadcast_to(local[:, j : j + 1], (LAT, 256)) for j in range(4)], axis=0)
        hit = one_hot(col == iota((UGRP, 256), 1))
        adv[pl.ds(r, UGRP), :] += mm(hit, tend[pl.ds(aligned, 256), :])

        @pl.when(lax.rem(g, 4) == 3)
        def _():
            out_copy(lax.div(g, 4)).start()

        return carry

    lax.fori_loop(0, COLS // UGRP, unpack, 0)
    for k in range(8):
        out_copy(k).wait()


ANY = pl.BlockSpec(memory_space=pl.ANY)
VM = pl.BlockSpec(memory_space=pltpu.VMEM)


def local(state, courant, diffusion, conv_mask, w_in, w_hidden, w_out):
    n_tx, n_ty = lax.axis_size("tx"), lax.axis_size("ty")
    ring = [(i, (i + 1) % n_tx) for i in range(n_tx)]
    line = [(i, i + 1) for i in range(n_ty - 1)]
    west = lax.ppermute(state[LON - 1], "tx", ring)
    east = lax.ppermute(state[0], "tx", [(j, i) for i, j in ring])
    south = lax.ppermute(state[:, LAT - 1], "ty", line)
    north = lax.ppermute(state[:, 0], "ty", [(j, i) for i, j in line])

    kept = (
        ((COLS, CH), F32),
        ((ROWS, CH), BF),
        ((ROWS, CH), BF),
        ((LAT, LON), I32),
        ((8, EDGE), I32),
        ((8, LON), I32),
        ((2 * LON + 2 * LAT, CH), F32),
        ((CH, HID), BF),
        ((3, HID, HID), BF),
        ((HID, CH), BF),
    )
    hidden = [pltpu.VMEM((TILE, HID), BF)] * 2
    held = pl.pallas_call(
        first_kernel,
        out_shape=[pltpu.VMEM(s, t) for s, t in kept],
        in_specs=[ANY] * 7,
        out_specs=[VM] * len(kept),
        scratch_shapes=[
            pltpu.VMEM((COLS + 2 * LAT + 8, CH), F32),
            pltpu.VMEM((COLS, CH), BF),
            pltpu.VMEM((LON, LAT), F32),
            pltpu.VMEM((LON, LAT), I32),
            pltpu.VMEM((LAT, LON), F32),
            pltpu.VMEM((LON, LON), F32),
            pltpu.VMEM((COLS // PGRP, PGRP), I32),
            pltpu.VMEM((PGRP, CH), F32),
            *hidden,
            pltpu.SMEM((8, LON), I32),
            pltpu.SemaphoreType.DMA((13,)),
            pltpu.SemaphoreType.DMA,
        ],
        compiler_params=pltpu.CompilerParams(vmem_limit_bytes=24 << 20),
        cost_estimate=pl.CostEstimate(flops=6_000_000_000, bytes_accessed=10 << 20, transcendentals=2 << 20),
        name="advance_pack",
    )(state.reshape(COLS, CH), courant.reshape(COLS, CH), diffusion, conv_mask, w_in, w_hidden, w_out)
    out = pl.pallas_call(
        second_kernel,
        out_shape=jax.ShapeDtypeStruct((COLS, CH), F32),
        in_specs=[VM] * 14,
        out_specs=ANY,
        scratch_shapes=[
            pltpu.VMEM((COLS, CH), F32),
            pltpu.VMEM((ROWS, CH), BF),
            pltpu.VMEM((ROWS, CH), BF),
            *hidden,
            pltpu.SMEM((8, LON), I32),
            pltpu.SemaphoreType.DMA,
            pltpu.SemaphoreType.DMA((8,)),
        ],
        compiler_params=pltpu.CompilerParams(vmem_limit_bytes=24 << 20),
        cost_estimate=pl.CostEstimate(flops=14_000_000_000, bytes_accessed=2 << 20, transcendentals=6 << 20),
        name="closure_unpack",
    )(west, east, south, north, *held)
    return out.reshape(LON, LAT, CH)


def solution(mesh):
    tile = P(("member", "tx"), "ty", None)
    flat = P(("member", "tx"), "ty")
    return jax.shard_map(
        local,
        mesh=mesh,
        in_specs=(tile, tile, flat, flat, P(), P(), P()),
        out_specs=tile,
        check_vma=False,
    )
```

```python
import functools

import jax
import jax.numpy as jnp
from jax import lax
from jax.experimental import pallas as pl
from jax.experimental.pallas import tpu as pltpu
from jax.sharding import PartitionSpec as P

LON, LAT, CH, HID = 128, 32, 128, 1024
COLS = LON * LAT
TILE = 512
CAP = 2048
ROWS = CAP + TILE
PGRP = 256
UGRP = 128
EDGE = 384
FIRST = 2
BF, F32, I32 = jnp.bfloat16, jnp.float32, jnp.int32


def iota(shape, dim):
    return lax.broadcasted_iota(I32, shape, dim)


def one_hot(hit):
    return jnp.where(hit, F32(1.0), F32(0.0)).astype(BF)


def mm(a, b):
    return jnp.dot(a, b, preferred_element_type=F32)


def silu(v):
    half = 0.5 * v
    return (half + half * jnp.tanh(half)).astype(BF)


def closure_tile(x, w_in, w_hid, w_out, ha, hb):
    step = 256

    def layer(src, weight, dst):
        for n in range(0, HID, step):
            dst[:, n : n + step] = silu(mm(src, weight(n)))

    layer(x, lambda n: w_in[:, n : n + step], ha)
    layer(ha[...], lambda n: w_hid[0, :, n : n + step], hb)
    layer(hb[...], lambda n: w_hid[1, :, n : n + step], ha)
    layer(ha[...], lambda n: w_hid[2, :, n : n + step], hb)
    return mm(hb[...], w_out[...]).astype(BF)


def append(packed, rows, aligned):
    n = rows.shape[0]
    head = packed[pl.ds(aligned, 16), :].astype(F32) + rows[:16]
    packed[pl.ds(aligned, 16), :] = head.astype(BF)
    packed[pl.ds(pl.multiple_of(aligned + 16, 16), n - 16), :] = rows[16:].astype(BF)


def align16(x):
    return pl.multiple_of((x // 16) * 16, 16)


def first_kernel(
    state_h, courant_h, diff_h, mask_h, win_h, whid_h, wout_h,
    adv, packed, tend, rank_t, rank_e, scal, coef, w_in, w_hid, w_out, lon_lo, lon_hi, lat_lo, lat_hi,
    st, cou, feat, dif, msk, rank_n, rank_r, ha, hb, scal_s, sem, sem_s,
):
    quarter = COLS // 4

    def in_copies(k):
        return (
            pltpu.make_async_copy(state_h.at[pl.ds(k * quarter, quarter)], st.at[pl.ds(k * quarter + LAT, quarter)], sem.at[k]),
            pltpu.make_async_copy(courant_h.at[pl.ds(k * quarter, quarter)], cou.at[pl.ds(k * quarter, quarter)], sem.at[4 + k]),
        )

    mask_copy = pltpu.make_async_copy(mask_h, msk, sem.at[8])
    diff_copy = pltpu.make_async_copy(diff_h, dif, sem.at[9])
    w_copies = (
        pltpu.make_async_copy(win_h, w_in, sem.at[10]),
        pltpu.make_async_copy(whid_h, w_hid, sem.at[11]),
        pltpu.make_async_copy(wout_h, w_out, sem.at[12]),
    )
    mask_copy.start()
    diff_copy.start()
    for k in range(4):
        for c in in_copies(k):
            c.start()
    for c in w_copies:
        c.start()
    packed[...] = jnp.zeros_like(packed)
    tend[...] = jnp.zeros_like(tend)
    st[0:LAT, :] = jnp.zeros((LAT, CH), F32)
    st[COLS + LAT : COLS + 2 * LAT, :] = jnp.zeros((LAT, CH), F32)

    mask_copy.wait()
    lat, lon = iota((LAT, LON), 0), iota((LAT, LON), 1)
    flags = msk[...]
    inner = (lon > 0) & (lon < LON - 1) & (lat > 0) & (lat < LAT - 1) & (flags == 1)
    inner_b = one_hot(inner)
    in_row = mm(one_hot(iota((LAT, LAT), 1) < iota((LAT, LAT), 0)), inner_b)
    per_lon = mm(jnp.ones((LAT, LAT), BF), inner_b).astype(BF)
    row_start = mm(per_lon, one_hot(iota((LON, LON), 0) < iota((LON, LON), 1)))
    rank = jnp.where(inner, in_row + row_start, F32(-4096.0))
    rank_t[...] = rank.astype(I32)
    starts = row_start[:1]
    flags_f = flags.astype(F32)
    lane = iota((1, LON), 1)
    ends = (lane == 0) | (lane == LON - 1)
    both = jnp.concatenate([rank, flags_f, jnp.zeros((LON - 2 * LAT, LON), F32)], axis=0)
    rank_n[...] = jnp.transpose(both)
    edge_row = jnp.concatenate(
        [
            rank_n[0:1, LAT : 2 * LAT],
            rank_n[LON - 1 :, LAT : 2 * LAT],
            jnp.zeros((1, 64), F32),
            jnp.where(ends, F32(0.0), flags_f[:1]),
            jnp.where(ends, F32(0.0), flags_f[LAT - 1 :]),
        ],
        axis=1,
    )
    edge_n = jnp.broadcast_to(jnp.sum(edge_row, axis=1, keepdims=True), (1, LON))
    scal[...] = jnp.where(iota((8, LON), 0) == 0, starts, edge_n).astype(I32)
    scal_copy = pltpu.make_async_copy(scal, scal_s, sem_s)
    scal_copy.start()
    rank_r[...] = jnp.concatenate(
        [rank_n[pl.ds(j, COLS // PGRP, stride=PGRP // LAT), :LAT] for j in range(PGRP // LAT)], axis=1
    ).astype(I32)
    edge_b = jnp.broadcast_to(edge_row, (16, EDGE)).astype(BF)
    edge_rank = mm(edge_b, one_hot(iota((EDGE, EDGE), 0) < iota((EDGE, EDGE), 1)))[:8]
    rank_e[...] = jnp.where(edge_row == 1.0, edge_rank + starts[:, LON - 1 :], F32(-4096.0)).astype(I32)
    diff_copy.wait()
    for c in in_copies(0):
        c.wait()

    lat_of = iota((LAT, CH), 0)
    low = iota((LAT, CH), 1) < 64

    def stencil(g, carry):
        k = lax.div(g, 4)

        @pl.when((lax.rem(g, 4) == 3) & (g < 15))
        def _():
            for c in in_copies(k + 1):
                c.wait()

        d8 = pltpu.roll(dif[...], lax.rem(LON - g * 8, LON), 1)
        for j in range(8):
            r = pl.multiple_of(g * PGRP + j * LAT, LAT)
            center = st[pl.ds(r + LAT, LAT), :]
            east = st[pl.ds(r + 2 * LAT, LAT), :]
            west = st[pl.ds(r, LAT), :]
            north = jnp.where(lat_of == LAT - 1, F32(0.0), st[pl.ds(r + LAT + 1, LAT), :])
            south = jnp.where(lat_of == 0, F32(0.0), st[pl.ds(r + LAT - 1, LAT), :])
            wind = 0.5 * cou[pl.ds(r, LAT), :].astype(F32)
            turned = pltpu.roll(wind, 64, 1)
            along_lon = jnp.where(low, wind, turned)
            along_lat = jnp.where(low, turned, wind)
            d = jnp.broadcast_to(d8[:, j : j + 1], (LAT, CH))
            laplace = east + west + north + south - 4.0 * center
            new = center - along_lon * (east - west) - along_lat * (north - south) + d * laplace
            adv[pl.ds(r, LAT), :] = new
            feat[pl.ds(r, LAT), :] = new.astype(BF)
            coef[pl.ds(g * 8 + j, 1), :] = (d - along_lat)[LAT - 1 :]
            coef[pl.ds(LON + g * 8 + j, 1), :] = (d + along_lat)[:1]
            if j == 0:

                @pl.when(g == 0)
                def _():
                    coef[2 * LON : 2 * LON + LAT, :] = d + along_lon

            if j == 7:

                @pl.when(g == 15)
                def _():
                    coef[2 * LON + LAT : 2 * LON + 2 * LAT, :] = d - along_lon

        return carry

    lax.fori_loop(0, 16, stencil, 0)
    lon_lo[...] = st[LAT : 2 * LAT, :]
    lon_hi[...] = st[COLS : COLS + LAT, :]
    lat_lo[...] = st[pl.ds(LAT, LON, stride=LAT), :]
    lat_hi[...] = st[pl.ds(2 * LAT - 1, LON, stride=LAT), :]
    scal_copy.wait()

    def pack(q, carry):
        todo = []
        for i in range(4):
            g = q * 4 + i
            aligned = align16(scal_s[0, g * 8])
            hits = iota((PGRP + 16, PGRP), 0) == rank_r[pl.ds(g, 1), :] - aligned
            todo.append((aligned, mm(one_hot(hits), feat[pl.ds(pl.multiple_of(g * PGRP, PGRP), PGRP), :])))
        for aligned, rows in todo:
            append(packed, rows, aligned)
        return carry

    lax.fori_loop(0, 4, pack, 0)
    for c in w_copies:
        c.wait()

    def tile(t, carry):
        r = pl.multiple_of(t * TILE, TILE)
        tend[pl.ds(r, TILE), :] = closure_tile(packed[pl.ds(r, TILE), :], w_in, w_hid, w_out, ha, hb)
        return carry

    lax.fori_loop(0, jnp.minimum(lax.div(scal_s[0, LON - 1], TILE), FIRST), tile, 0)


def middle_kernel(packed, scal, w_in, w_hid, w_out, tend, ha, hb, scal_s, sem_s):
    scal_copy = pltpu.make_async_copy(scal, scal_s, sem_s)
    scal_copy.start()
    scal_copy.wait()
    tend[...] = jnp.zeros_like(tend)

    @pl.when(scal_s[0, LON - 1] >= (FIRST + 1) * TILE)
    def _():
        x = packed[FIRST * TILE : (FIRST + 1) * TILE, :]
        tend[...] = closure_tile(x, w_in, w_hid, w_out, ha, hb)


def last_kernel(
    west, east, south, north, adv_i, packed_i, tend_i, tend_m, rank_t, rank_e, scal, coef, w_in, w_hid, w_out,
    out_h, adv, packed, tend, ha, hb, scal_s, sem_s, sem,
):
    scal_copy = pltpu.make_async_copy(scal, scal_s, sem_s)
    scal_copy.start()
    adv[...] = adv_i[...]
    packed[...] = packed_i[...]
    tend[: FIRST * TILE, :] = tend_i[...]
    tend[FIRST * TILE : (FIRST + 1) * TILE, :] = tend_m[...]
    tend[(FIRST + 1) * TILE :, :] = jnp.zeros((ROWS - (FIRST + 1) * TILE, CH), BF)
    adv[0:LAT, :] += west[...] * coef[2 * LON : 2 * LON + LAT, :]
    adv[COLS - LAT :, :] += east[...] * coef[2 * LON + LAT :, :]
    low, high = pl.ds(0, LON, stride=LAT), pl.ds(LAT - 1, LON, stride=LAT)
    adv[high, :] = adv[high, :] + north[...] * coef[:LON, :]
    adv[low, :] = adv[low, :] + south[...] * coef[LON : 2 * LON, :]
    edge = jnp.concatenate(
        [adv[0:LAT, :], adv[COLS - LAT :, :], jnp.zeros((64, CH), F32), adv[low, :], adv[high, :]], axis=0
    ).astype(BF)
    scal_copy.wait()
    inner_n = scal_s[0, LON - 1]
    count = inner_n + scal_s[1, 0]
    aligned_e = align16(inner_n)
    hits = iota((320 + 16, EDGE), 0) == rank_e[:1, :] - aligned_e
    append(packed, mm(one_hot(hits), edge), aligned_e)

    def tile(t, carry):
        r = pl.multiple_of(t * TILE, TILE)
        tend[pl.ds(r, TILE), :] = closure_tile(packed[pl.ds(r, TILE), :], w_in, w_hid, w_out, ha, hb)
        return carry

    done = jnp.minimum(lax.div(inner_n, TILE), FIRST + 1)
    lax.fori_loop(done, lax.div(count + TILE - 1, TILE), tile, 0)

    rank_col = jnp.concatenate(
        [jnp.transpose(jnp.broadcast_to(rank_e[:1, k * 128 : k * 128 + 128], (128, 128))) for k in range(3)], axis=0
    )
    picks = jnp.concatenate([rank_col - aligned_e - 128 * k for k in range(3)], axis=1) == (
        iota((EDGE, EDGE), 1) & 127
    )
    back = mm(one_hot(picks), tend[pl.ds(aligned_e, EDGE), :])
    adv[0:LAT, :] += back[0:LAT]
    adv[COLS - LAT :, :] += back[LAT : 2 * LAT]
    adv[low, :] = adv[low, :] + back[128:256]
    adv[high, :] = adv[high, :] + back[256:384]

    def out_copy(k):
        part = pl.ds(k * (COLS // 8), COLS // 8)
        return pltpu.make_async_copy(adv.at[part], out_h.at[part], sem.at[k])

    def unpack(q, carry):
        turned = pltpu.roll(rank_t[...], lax.rem(LON - q * 16, LON), 1)
        todo = []
        for i in range(4):
            aligned = align16(scal_s[0, q * 16 + 4 * i])
            cols = [jnp.broadcast_to(turned[:, 4 * i + j : 4 * i + j + 1], (LAT, 256)) for j in range(4)]
            hit = one_hot(jnp.concatenate(cols, axis=0) == iota((UGRP, 256), 1) + aligned)
            todo.append(mm(hit, tend[pl.ds(aligned, 256), :]))
        r = pl.multiple_of(q * 4 * UGRP, 4 * UGRP)
        adv[pl.ds(r, 4 * UGRP), :] += jnp.concatenate(todo, axis=0)
        out_copy(q).start()
        return carry

    lax.fori_loop(0, 8, unpack, 0)
    for k in range(8):
        out_copy(k).wait()


ANY = pl.BlockSpec(memory_space=pl.ANY)
HBM = pl.BlockSpec(memory_space=pltpu.HBM)
VM = pl.BlockSpec(memory_space=pltpu.VMEM)


def in_hbm(x):
    return pltpu.with_memory_space_constraint(x, pltpu.HBM)


def params():
    return pltpu.CompilerParams(vmem_limit_bytes=24 << 20)


def cost(gflops):
    return pl.CostEstimate(flops=gflops * 10**9, bytes_accessed=1 << 20, transcendentals=1 << 20)


def local(state, courant, diffusion, conv_mask, w_in, w_hidden, w_out):
    n_tx, n_ty = lax.axis_size("tx"), lax.axis_size("ty")
    ring = [(i, (i + 1) % n_tx) for i in range(n_tx)]
    line = [(i, i + 1) for i in range(n_ty - 1)]
    kept = (
        ((COLS, CH), F32),
        ((ROWS, CH), BF),
        ((FIRST * TILE, CH), BF),
        ((LAT, LON), I32),
        ((8, EDGE), I32),
        ((8, LON), I32),
        ((2 * LON + 2 * LAT, CH), F32),
        ((CH, HID), BF),
        ((3, HID, HID), BF),
        ((HID, CH), BF),
        ((LAT, CH), F32),
        ((LAT, CH), F32),
        ((LON, CH), F32),
        ((LON, CH), F32),
    )
    hidden = [pltpu.VMEM((TILE, HID), BF)] * 2
    smem = [pltpu.SMEM((8, LON), I32)]
    held = pl.pallas_call(
        first_kernel,
        out_shape=[pltpu.VMEM(s, t) for s, t in kept],
        in_specs=[HBM] * 7,
        out_specs=[VM] * len(kept),
        scratch_shapes=[
            pltpu.VMEM((COLS + 2 * LAT + 8, CH), F32),
            pltpu.VMEM((COLS, CH), BF),
            pltpu.VMEM((COLS, CH), BF),
            pltpu.VMEM((LAT, LON), F32),
            pltpu.VMEM((LAT, LON), I32),
            pltpu.VMEM((LON, LON), F32),
            pltpu.VMEM((COLS // PGRP, PGRP), I32),
            *hidden,
            *smem,
            pltpu.SemaphoreType.DMA((13,)),
            pltpu.SemaphoreType.DMA,
        ],
        compiler_params=params(),
        cost_estimate=cost(9),
        name="advance_pack",
    )(*map(in_hbm, (state.reshape(COLS, CH), courant.reshape(COLS, CH), diffusion.T, conv_mask.T, w_in, w_hidden, w_out)))
    adv, packed, tend, rank_t, rank_e, scal, coef, w_in, w_hid, w_out, lon_lo, lon_hi, lat_lo, lat_hi = held
    west = lax.ppermute(lon_hi, "tx", ring)
    east = lax.ppermute(lon_lo, "tx", [(j, i) for i, j in ring])
    south = lax.ppermute(lat_hi, "ty", line)
    north = lax.ppermute(lat_lo, "ty", [(j, i) for i, j in line])
    middle = pl.pallas_call(
        middle_kernel,
        out_shape=pltpu.VMEM((TILE, CH), BF),
        in_specs=[VM] * 5,
        out_specs=VM,
        scratch_shapes=[*hidden, *smem, pltpu.SemaphoreType.DMA],
        compiler_params=params(),
        cost_estimate=cost(4),
        name="closure_middle",
    )(packed, scal, w_in, w_hid, w_out)
    out = pl.pallas_call(
        last_kernel,
        out_shape=jax.ShapeDtypeStruct((COLS, CH), F32),
        in_specs=[VM] * 15,
        out_specs=HBM,
        scratch_shapes=[
            pltpu.VMEM((COLS, CH), F32),
            pltpu.VMEM((ROWS, CH), BF),
            pltpu.VMEM((ROWS, CH), BF),
            *hidden,
            *smem,
            pltpu.SemaphoreType.DMA,
            pltpu.SemaphoreType.DMA((8,)),
        ],
        compiler_params=params(),
        cost_estimate=cost(4),
        name="closure_unpack",
    )(west, east, south, north, adv, packed, tend, middle, rank_t, rank_e, scal, coef, w_in, w_hid, w_out)
    return out.reshape(LON, LAT, CH)


def solution(mesh):
    tile = P(("member", "tx"), "ty", None)
    flat = P(("member", "tx"), "ty")
    return jax.shard_map(
        local,
        mesh=mesh,
        in_specs=(tile, tile, flat, flat, P(), P(), P()),
        out_specs=tile,
        check_vma=False,
    )
```

```python
import functools

import jax
import jax.numpy as jnp
from jax import lax
from jax.experimental import pallas as pl
from jax.experimental.pallas import tpu as pltpu
from jax.sharding import PartitionSpec as P

LON, LAT, CH, HID = 128, 32, 128, 1024
COLS = LON * LAT
TILE = 512
CAP = 2048
ROWS = CAP + TILE
PGRP = 256
UGRP = 128
EDGE = 384
FIRST = 3
BF, F32, I32 = jnp.bfloat16, jnp.float32, jnp.int32


def iota(shape, dim):
    return lax.broadcasted_iota(I32, shape, dim)


def one_hot(hit):
    return jnp.where(hit, F32(1.0), F32(0.0)).astype(BF)


def mm(a, b):
    return jnp.dot(a, b, preferred_element_type=F32)


def silu(v):
    half = 0.5 * v
    return (half + half * jnp.tanh(half)).astype(BF)


def closure_tile(x, w_in, w_hid, w_out, ha, hb):
    step = 256

    def layer(src, weight, dst):
        for n in range(0, HID, step):
            dst[:, n : n + step] = silu(mm(src, weight(n)))

    layer(x, lambda n: w_in[:, n : n + step], ha)
    layer(ha[...], lambda n: w_hid[0, :, n : n + step], hb)
    layer(hb[...], lambda n: w_hid[1, :, n : n + step], ha)
    layer(ha[...], lambda n: w_hid[2, :, n : n + step], hb)
    return mm(hb[...], w_out[...]).astype(BF)


def append(packed, rows, aligned):
    n = rows.shape[0]
    head = packed[pl.ds(aligned, 16), :].astype(F32) + rows[:16]
    packed[pl.ds(aligned, 16), :] = head.astype(BF)
    packed[pl.ds(pl.multiple_of(aligned + 16, 16), n - 16), :] = rows[16:].astype(BF)


def align16(x):
    return pl.multiple_of((x // 16) * 16, 16)


def first_kernel(
    state_h, courant_h, diff_h, mask_h, win_h, whid_h, wout_h,
    adv, packed, rank_t, rank_e, scal, coef, w_in, w_hid, w_out, lon_lo, lon_hi, lat_lo, lat_hi,
    st, cou, feat, dif, msk, rank_n, rank_r, scal_s, sem, sem_s,
):
    quarter = COLS // 4

    def in_copies(k):
        return (
            pltpu.make_async_copy(state_h.at[pl.ds(k * quarter, quarter)], st.at[pl.ds(k * quarter + LAT, quarter)], sem.at[k]),
            pltpu.make_async_copy(courant_h.at[pl.ds(k * quarter, quarter)], cou.at[pl.ds(k * quarter, quarter)], sem.at[4 + k]),
        )

    mask_copy = pltpu.make_async_copy(mask_h, msk, sem.at[8])
    diff_copy = pltpu.make_async_copy(diff_h, dif, sem.at[9])
    w_copies = (
        pltpu.make_async_copy(win_h, w_in, sem.at[10]),
        pltpu.make_async_copy(whid_h, w_hid, sem.at[11]),
        pltpu.make_async_copy(wout_h, w_out, sem.at[12]),
    )
    mask_copy.start()
    diff_copy.start()
    for k in range(4):
        for c in in_copies(k):
            c.start()
    for c in w_copies:
        c.start()
    packed[...] = jnp.zeros_like(packed)
    st[0:LAT, :] = jnp.zeros((LAT, CH), F32)
    st[COLS + LAT : COLS + 2 * LAT, :] = jnp.zeros((LAT, CH), F32)

    mask_copy.wait()
    lat, lon = iota((LAT, LON), 0), iota((LAT, LON), 1)
    flags = msk[...]
    inner = (lon > 0) & (lon < LON - 1) & (lat > 0) & (lat < LAT - 1) & (flags == 1)
    inner_b = one_hot(inner)
    in_row = mm(one_hot(iota((LAT, LAT), 1) < iota((LAT, LAT), 0)), inner_b)
    per_lon = mm(jnp.ones((LAT, LAT), BF), inner_b).astype(BF)
    row_start = mm(per_lon, one_hot(iota((LON, LON), 0) < iota((LON, LON), 1)))
    rank = jnp.where(inner, in_row + row_start, F32(-4096.0))
    rank_t[...] = rank.astype(I32)
    starts = row_start[:1]
    flags_f = flags.astype(F32)
    lane = iota((1, LON), 1)
    ends = (lane == 0) | (lane == LON - 1)
    both = jnp.concatenate([rank, flags_f, jnp.zeros((LON - 2 * LAT, LON), F32)], axis=0)
    rank_n[...] = jnp.transpose(both)
    edge_row = jnp.concatenate(
        [
            rank_n[0:1, LAT : 2 * LAT],
            rank_n[LON - 1 :, LAT : 2 * LAT],
            jnp.zeros((1, 64), F32),
            jnp.where(ends, F32(0.0), flags_f[:1]),
            jnp.where(ends, F32(0.0), flags_f[LAT - 1 :]),
        ],
        axis=1,
    )
    edge_n = jnp.broadcast_to(jnp.sum(edge_row, axis=1, keepdims=True), (1, LON))
    scal[...] = jnp.where(iota((8, LON), 0) == 0, starts, edge_n).astype(I32)
    scal_copy = pltpu.make_async_copy(scal, scal_s, sem_s)
    scal_copy.start()
    rank_r[...] = jnp.concatenate(
        [rank_n[pl.ds(j, COLS // PGRP, stride=PGRP // LAT), :LAT] for j in range(PGRP // LAT)], axis=1
    ).astype(I32)
    edge_b = jnp.broadcast_to(edge_row, (16, EDGE)).astype(BF)
    edge_rank = mm(edge_b, one_hot(iota((EDGE, EDGE), 0) < iota((EDGE, EDGE), 1)))[:8]
    rank_e[...] = jnp.where(edge_row == 1.0, edge_rank + starts[:, LON - 1 :], F32(-4096.0)).astype(I32)
    diff_copy.wait()
    for c in in_copies(0):
        c.wait()

    lat_of = iota((LAT, CH), 0)
    low = iota((LAT, CH), 1) < 64

    def stencil(g, carry):
        k = lax.div(g, 4)

        @pl.when((lax.rem(g, 4) == 3) & (g < 15))
        def _():
            for c in in_copies(k + 1):
                c.wait()

        d8 = pltpu.roll(dif[...], lax.rem(LON - g * 8, LON), 1)
        for j in range(8):
            r = pl.multiple_of(g * PGRP + j * LAT, LAT)
            center = st[pl.ds(r + LAT, LAT), :]
            east = st[pl.ds(r + 2 * LAT, LAT), :]
            west = st[pl.ds(r, LAT), :]
            north = jnp.where(lat_of == LAT - 1, F32(0.0), st[pl.ds(r + LAT + 1, LAT), :])
            south = jnp.where(lat_of == 0, F32(0.0), st[pl.ds(r + LAT - 1, LAT), :])
            wind = 0.5 * cou[pl.ds(r, LAT), :].astype(F32)
            turned = pltpu.roll(wind, 64, 1)
            along_lon = jnp.where(low, wind, turned)
            along_lat = jnp.where(low, turned, wind)
            d = jnp.broadcast_to(d8[:, j : j + 1], (LAT, CH))
            laplace = east + west + north + south - 4.0 * center
            new = center - along_lon * (east - west) - along_lat * (north - south) + d * laplace
            adv[pl.ds(r, LAT), :] = new
            feat[pl.ds(r, LAT), :] = new.astype(BF)
            coef[pl.ds(g * 8 + j, 1), :] = (d - along_lat)[LAT - 1 :]
            coef[pl.ds(LON + g * 8 + j, 1), :] = (d + along_lat)[:1]
            if j == 0:

                @pl.when(g == 0)
                def _():
                    coef[2 * LON : 2 * LON + LAT, :] = d + along_lon

            if j == 7:

                @pl.when(g == 15)
                def _():
                    coef[2 * LON + LAT : 2 * LON + 2 * LAT, :] = d - along_lon

        return carry

    lax.fori_loop(0, 16, stencil, 0)
    lon_lo[...] = st[LAT : 2 * LAT, :]
    lon_hi[...] = st[COLS : COLS + LAT, :]
    lat_lo[...] = st[pl.ds(LAT, LON, stride=LAT), :]
    lat_hi[...] = st[pl.ds(2 * LAT - 1, LON, stride=LAT), :]
    scal_copy.wait()

    def pack(q, carry):
        todo = []
        for i in range(4):
            g = q * 4 + i
            aligned = align16(scal_s[0, g * 8])
            hits = iota((PGRP + 16, PGRP), 0) == rank_r[pl.ds(g, 1), :] - aligned
            todo.append((aligned, mm(one_hot(hits), feat[pl.ds(pl.multiple_of(g * PGRP, PGRP), PGRP), :])))
        for aligned, rows in todo:
            append(packed, rows, aligned)
        return carry

    lax.fori_loop(0, 4, pack, 0)
    for c in w_copies:
        c.wait()


def tiles_of(packed, tend, weights, hidden, first, end):
    def tile(t, carry):
        r = pl.multiple_of(t * TILE, TILE)
        tend[pl.ds(r, TILE), :] = closure_tile(packed[pl.ds(r, TILE), :], *weights, *hidden)
        return carry

    lax.fori_loop(first, end, tile, 0)


def middle_kernel(packed, scal, w_in, w_hid, w_out, tend, ha, hb, scal_s, sem_s):
    scal_copy = pltpu.make_async_copy(scal, scal_s, sem_s)
    scal_copy.start()
    tend[...] = jnp.zeros_like(tend)
    scal_copy.wait()
    end = jnp.minimum(lax.div(scal_s[0, LON - 1], TILE), FIRST)
    tiles_of(packed, tend, (w_in, w_hid, w_out), (ha, hb), 0, end)


def last_kernel(
    west, east, south, north, adv_i, packed_i, tend_i, rank_t, rank_e, scal, coef, w_in, w_hid, w_out,
    out_h, adv, packed, tend, ha, hb, scal_s, sem_s, sem,
):
    scal_copy = pltpu.make_async_copy(scal, scal_s, sem_s)
    scal_copy.start()
    adv[...] = adv_i[...]
    packed[...] = packed_i[...]
    tend[: FIRST * TILE, :] = tend_i[...]
    tend[FIRST * TILE :, :] = jnp.zeros((ROWS - FIRST * TILE, CH), BF)
    adv[0:LAT, :] += west[...] * coef[2 * LON : 2 * LON + LAT, :]
    adv[COLS - LAT :, :] += east[...] * coef[2 * LON + LAT :, :]
    low, high = pl.ds(0, LON, stride=LAT), pl.ds(LAT - 1, LON, stride=LAT)
    adv[high, :] = adv[high, :] + north[...] * coef[:LON, :]
    adv[low, :] = adv[low, :] + south[...] * coef[LON : 2 * LON, :]
    edge = jnp.concatenate(
        [adv[0:LAT, :], adv[COLS - LAT :, :], jnp.zeros((64, CH), F32), adv[low, :], adv[high, :]], axis=0
    ).astype(BF)
    scal_copy.wait()
    inner_n = scal_s[0, LON - 1]
    count = inner_n + scal_s[1, 0]
    aligned_e = align16(inner_n)
    hits = iota((320 + 16, EDGE), 0) == rank_e[:1, :] - aligned_e
    append(packed, mm(one_hot(hits), edge), aligned_e)

    done = jnp.minimum(lax.div(inner_n, TILE), FIRST)
    tiles_of(packed, tend, (w_in, w_hid, w_out), (ha, hb), done, lax.div(count + TILE - 1, TILE))

    rank_col = jnp.concatenate(
        [jnp.transpose(jnp.broadcast_to(rank_e[:1, k * 128 : k * 128 + 128], (128, 128))) for k in range(3)], axis=0
    )
    picks = jnp.concatenate([rank_col - aligned_e - 128 * k for k in range(3)], axis=1) == (
        iota((EDGE, EDGE), 1) & 127
    )
    back = mm(one_hot(picks), tend[pl.ds(aligned_e, EDGE), :])
    adv[0:LAT, :] += back[0:LAT]
    adv[COLS - LAT :, :] += back[LAT : 2 * LAT]
    adv[low, :] = adv[low, :] + back[128:256]
    adv[high, :] = adv[high, :] + back[256:384]

    def out_copy(k):
        part = pl.ds(k * (COLS // 8), COLS // 8)
        return pltpu.make_async_copy(adv.at[part], out_h.at[part], sem.at[k])

    def unpack(q, carry):
        turned = pltpu.roll(rank_t[...], lax.rem(LON - q * 16, LON), 1)
        todo = []
        for i in range(4):
            aligned = align16(scal_s[0, q * 16 + 4 * i])
            cols = [jnp.broadcast_to(turned[:, 4 * i + j : 4 * i + j + 1], (LAT, 256)) for j in range(4)]
            hit = one_hot(jnp.concatenate(cols, axis=0) == iota((UGRP, 256), 1) + aligned)
            todo.append(mm(hit, tend[pl.ds(aligned, 256), :]))
        r = pl.multiple_of(q * 4 * UGRP, 4 * UGRP)
        adv[pl.ds(r, 4 * UGRP), :] += jnp.concatenate(todo, axis=0)
        out_copy(q).start()
        return carry

    lax.fori_loop(0, 8, unpack, 0)
    for k in range(8):
        out_copy(k).wait()


ANY = pl.BlockSpec(memory_space=pl.ANY)
HBM = pl.BlockSpec(memory_space=pltpu.HBM)
VM = pl.BlockSpec(memory_space=pltpu.VMEM)


def in_hbm(x):
    return pltpu.with_memory_space_constraint(x, pltpu.HBM)


def params():
    return pltpu.CompilerParams(vmem_limit_bytes=24 << 20)


def cost(gflops):
    return pl.CostEstimate(flops=gflops * 10**9, bytes_accessed=1 << 20, transcendentals=1 << 20)


def local(state, courant, diffusion, conv_mask, w_in, w_hidden, w_out):
    n_tx, n_ty = lax.axis_size("tx"), lax.axis_size("ty")
    ring = [(i, (i + 1) % n_tx) for i in range(n_tx)]
    line = [(i, i + 1) for i in range(n_ty - 1)]
    kept = (
        ((COLS, CH), F32),
        ((ROWS, CH), BF),
        ((LAT, LON), I32),
        ((8, EDGE), I32),
        ((8, LON), I32),
        ((2 * LON + 2 * LAT, CH), F32),
        ((CH, HID), BF),
        ((3, HID, HID), BF),
        ((HID, CH), BF),
        ((LAT, CH), F32),
        ((LAT, CH), F32),
        ((LON, CH), F32),
        ((LON, CH), F32),
    )
    hidden = [pltpu.VMEM((TILE, HID), BF)] * 2
    smem = [pltpu.SMEM((8, LON), I32)]
    held = pl.pallas_call(
        first_kernel,
        out_shape=[pltpu.VMEM(s, t) for s, t in kept],
        in_specs=[HBM] * 7,
        out_specs=[VM] * len(kept),
        scratch_shapes=[
            pltpu.VMEM((COLS + 2 * LAT + 8, CH), F32),
            pltpu.VMEM((COLS, CH), BF),
            pltpu.VMEM((COLS, CH), BF),
            pltpu.VMEM((LAT, LON), F32),
            pltpu.VMEM((LAT, LON), I32),
            pltpu.VMEM((LON, LON), F32),
            pltpu.VMEM((COLS // PGRP, PGRP), I32),
            *smem,
            pltpu.SemaphoreType.DMA((13,)),
            pltpu.SemaphoreType.DMA,
        ],
        compiler_params=params(),
        cost_estimate=cost(1),
        name="advance_pack",
    )(*map(in_hbm, (state.reshape(COLS, CH), courant.reshape(COLS, CH), diffusion.T, conv_mask.T, w_in, w_hidden, w_out)))
    adv, packed, rank_t, rank_e, scal, coef, w_in, w_hid, w_out, lon_lo, lon_hi, lat_lo, lat_hi = held
    west = lax.ppermute(lon_hi, "tx", ring)
    east = lax.ppermute(lon_lo, "tx", [(j, i) for i, j in ring])
    south = lax.ppermute(lat_hi, "ty", line)
    north = lax.ppermute(lat_lo, "ty", [(j, i) for i, j in line])
    tend = pl.pallas_call(
        middle_kernel,
        out_shape=pltpu.VMEM((FIRST * TILE, CH), BF),
        in_specs=[VM] * 5,
        out_specs=VM,
        scratch_shapes=[*hidden, *smem, pltpu.SemaphoreType.DMA],
        compiler_params=params(),
        cost_estimate=cost(12),
        name="closure_middle",
    )(packed, scal, w_in, w_hid, w_out)
    out = pl.pallas_call(
        last_kernel,
        out_shape=jax.ShapeDtypeStruct((COLS, CH), F32),
        in_specs=[VM] * 14,
        out_specs=HBM,
        scratch_shapes=[
            pltpu.VMEM((COLS, CH), F32),
            pltpu.VMEM((ROWS, CH), BF),
            pltpu.VMEM((ROWS, CH), BF),
            *hidden,
            *smem,
            pltpu.SemaphoreType.DMA,
            pltpu.SemaphoreType.DMA((8,)),
        ],
        compiler_params=params(),
        cost_estimate=cost(4),
        name="closure_unpack",
    )(west, east, south, north, adv, packed, tend, rank_t, rank_e, scal, coef, w_in, w_hid, w_out)
    return out.reshape(LON, LAT, CH)


def solution(mesh):
    tile = P(("member", "tx"), "ty", None)
    flat = P(("member", "tx"), "ty")
    return jax.shard_map(
        local,
        mesh=mesh,
        in_specs=(tile, tile, flat, flat, P(), P(), P()),
        out_specs=tile,
        check_vma=False,
    )
```

```python
import functools

import jax
import jax.numpy as jnp
from jax import lax
from jax.experimental import pallas as pl
from jax.experimental.pallas import tpu as pltpu
from jax.sharding import PartitionSpec as P

LON, LAT, CH, HID = 128, 32, 128, 1024
COLS = LON * LAT
TILE = 512
CAP = 2048
ROWS = CAP + TILE
PGRP = 256
UGRP = 128
EDGE = 384
EARLY = 6
FIRST = 3
BF, F32, I32 = jnp.bfloat16, jnp.float32, jnp.int32


def iota(shape, dim):
    return lax.broadcasted_iota(I32, shape, dim)


def one_hot(hit):
    return jnp.where(hit, F32(1.0), F32(0.0)).astype(BF)


def mm(a, b):
    return jnp.dot(a, b, preferred_element_type=F32)


def silu(v):
    half = 0.5 * v
    return (half + half * jnp.tanh(half)).astype(BF)


def closure_tile(x, w_in, w_hid, w_out, ha, hb, beside=()):
    step = 256
    beside = list(beside)

    def layer(src, weight, dst, side):
        for n in range(0, HID, step):
            dst[:, n : n + step] = silu(mm(src, weight(n)))
            if side and n in (0, 512) and beside:
                beside.pop(0)()

    layer(x, lambda n: w_in[:, n : n + step], ha, False)
    layer(ha[...], lambda n: w_hid[0, :, n : n + step], hb, True)
    layer(hb[...], lambda n: w_hid[1, :, n : n + step], ha, True)
    layer(ha[...], lambda n: w_hid[2, :, n : n + step], hb, True)
    return mm(hb[...], w_out[...]).astype(BF)


def append(packed, rows, aligned):
    n = rows.shape[0]
    head = packed[pl.ds(aligned, 16), :].astype(F32) + rows[:16]
    packed[pl.ds(aligned, 16), :] = head.astype(BF)
    packed[pl.ds(pl.multiple_of(aligned + 16, 16), n - 16), :] = rows[16:].astype(BF)


def align16(x):
    return pl.multiple_of((x // 16) * 16, 16)


def first_kernel(
    state_h, courant_h, diff_h, mask_h, win_h, whid_h, wout_h,
    adv, packed, tend, rank_t, rank_e, scal, coef, w_in, w_hid, w_out, lon_lo, lon_hi, lat_lo, lat_hi,
    st, cou, feat, dif, dif_n, msk, rank_n, rank_r, ha, hb, scal_s, sem, sem_s,
):
    quarter = COLS // 4

    def in_copies(k):
        return (
            pltpu.make_async_copy(state_h.at[pl.ds(k * quarter, quarter)], st.at[pl.ds(k * quarter + LAT, quarter)], sem.at[k]),
            pltpu.make_async_copy(courant_h.at[pl.ds(k * quarter, quarter)], cou.at[pl.ds(k * quarter, quarter)], sem.at[4 + k]),
        )

    mask_copy = pltpu.make_async_copy(mask_h, msk, sem.at[8])
    diff_copy = pltpu.make_async_copy(diff_h, dif, sem.at[9])
    w_copies = (
        pltpu.make_async_copy(win_h, w_in, sem.at[10]),
        pltpu.make_async_copy(whid_h, w_hid, sem.at[11]),
        pltpu.make_async_copy(wout_h, w_out, sem.at[12]),
    )
    mask_copy.start()
    diff_copy.start()
    for k in range(4):
        for c in in_copies(k):
            c.start()
    for c in w_copies:
        c.start()
    packed[...] = jnp.zeros_like(packed)
    st[0:LAT, :] = jnp.zeros((LAT, CH), F32)
    st[COLS + LAT : COLS + 2 * LAT, :] = jnp.zeros((LAT, CH), F32)

    mask_copy.wait()
    lat, lon = iota((LAT, LON), 0), iota((LAT, LON), 1)
    flags = msk[...]
    inner = (lon > 0) & (lon < LON - 1) & (lat > 0) & (lat < LAT - 1) & (flags == 1)
    inner_b = one_hot(inner)
    in_row = mm(one_hot(iota((LAT, LAT), 1) < iota((LAT, LAT), 0)), inner_b)
    per_lon = mm(jnp.ones((LAT, LAT), BF), inner_b).astype(BF)
    row_start = mm(per_lon, one_hot(iota((LON, LON), 0) < iota((LON, LON), 1)))
    rank = jnp.where(inner, in_row + row_start, F32(-4096.0))
    rank_t[...] = rank.astype(I32)
    starts = row_start[:1]
    flags_f = flags.astype(F32)
    lane = iota((1, LON), 1)
    ends = (lane == 0) | (lane == LON - 1)
    both = jnp.concatenate([rank, flags_f, jnp.zeros((LON - 2 * LAT, LON), F32)], axis=0)
    rank_n[...] = jnp.transpose(both)
    edge_row = jnp.concatenate(
        [
            rank_n[0:1, LAT : 2 * LAT],
            rank_n[LON - 1 :, LAT : 2 * LAT],
            jnp.zeros((1, 64), F32),
            jnp.where(ends, F32(0.0), flags_f[:1]),
            jnp.where(ends, F32(0.0), flags_f[LAT - 1 :]),
        ],
        axis=1,
    )
    edge_n = jnp.broadcast_to(jnp.sum(edge_row, axis=1, keepdims=True), (1, LON))
    scal[...] = jnp.where(iota((8, LON), 0) == 0, starts, edge_n).astype(I32)
    scal_copy = pltpu.make_async_copy(scal, scal_s, sem_s)
    scal_copy.start()
    rank_r[...] = jnp.concatenate(
        [rank_n[pl.ds(j, COLS // PGRP, stride=PGRP // LAT), :LAT] for j in range(PGRP // LAT)], axis=1
    ).astype(I32)
    edge_b = jnp.broadcast_to(edge_row, (16, EDGE)).astype(BF)
    edge_rank = mm(edge_b, one_hot(iota((EDGE, EDGE), 0) < iota((EDGE, EDGE), 1)))[:8]
    rank_e[...] = jnp.where(edge_row == 1.0, edge_rank + starts[:, LON - 1 :], F32(-4096.0)).astype(I32)
    diff_copy.wait()
    for c in in_copies(0):
        c.wait()

    dif_1 = dif[...].astype(BF).astype(F32)
    dif_2 = (dif[...] - dif_1).astype(BF).astype(F32)
    dif_3 = dif[...] - dif_1 - dif_2
    dif_n[...] = jnp.transpose(jnp.concatenate([dif_1, dif_2, dif_3, jnp.zeros((LAT, LON), F32)], axis=0))

    lat_of = iota((LAT, CH), 0)
    low = iota((LAT, CH), 1) < 64
    own_lat = (iota((LAT, CH), 1) & 31) == lat_of
    ones = jnp.ones((CH, CH), BF)

    def stencil(i):
        spread = [jnp.where(own_lat, dif_n[pl.ds(i * 16 + j, 1), :], F32(0.0)) for j in range(16)]
        d_all = mm(jnp.concatenate(spread, axis=0).astype(BF), ones)
        for j in range(16):
            r = pl.multiple_of(i * 2 * PGRP + j * LAT, LAT)
            center = st[pl.ds(r + LAT, LAT), :]
            east = st[pl.ds(r + 2 * LAT, LAT), :]
            west = st[pl.ds(r, LAT), :]
            north = jnp.where(lat_of == LAT - 1, F32(0.0), st[pl.ds(r + LAT + 1, LAT), :])
            south = jnp.where(lat_of == 0, F32(0.0), st[pl.ds(r + LAT - 1, LAT), :])
            wind = 0.5 * cou[pl.ds(r, LAT), :].astype(F32)
            turned = pltpu.roll(wind, 64, 1)
            along_lon = jnp.where(low, wind, turned)
            along_lat = jnp.where(low, turned, wind)
            d = d_all[j * LAT : (j + 1) * LAT]
            laplace = east + west + north + south - 4.0 * center
            new = center - along_lon * (east - west) - along_lat * (north - south) + d * laplace
            adv[pl.ds(r, LAT), :] = new
            feat[pl.ds(r, LAT), :] = new.astype(BF)
            coef[pl.ds(i * 16 + j, 1), :] = (d - along_lat)[LAT - 1 :]
            coef[pl.ds(LON + i * 16 + j, 1), :] = (d + along_lat)[:1]
            if isinstance(i, int) and i == 0 and j == 0:
                coef[2 * LON : 2 * LON + LAT, :] = d + along_lon
            if isinstance(i, int) and i == 7 and j == 15:
                coef[2 * LON + LAT : 2 * LON + 2 * LAT, :] = d - along_lon

    def pack(i):
        todo = []
        for k in range(2):
            g = i * 2 + k
            aligned = align16(scal_s[0, g * 8])
            hits = iota((PGRP + 16, PGRP), 0) == rank_r[pl.ds(g, 1), :] - aligned
            todo.append((aligned, mm(one_hot(hits), feat[pl.ds(pl.multiple_of(g * PGRP, PGRP), PGRP), :])))
        for aligned, rows in todo:
            append(packed, rows, aligned)

    def wait_quarter(k):
        for c in in_copies(k):
            c.wait()

    wait_quarter(1)
    scal_copy.wait()
    stencil(0)

    def both_steps(i, carry):
        @pl.when((lax.rem(i, 2) == 1) & (i > 1))
        def _():
            wait_quarter(lax.div(i, 2) + 1)

        stencil(i)
        pack(i - 1)
        return carry

    lax.fori_loop(1, 7, both_steps, 0)
    stencil(7)
    pack(6)
    pack(7)
    lon_lo[...] = st[LAT : 2 * LAT, :]
    lon_hi[...] = st[COLS : COLS + LAT, :]
    lat_lo[...] = st[pl.ds(LAT, LON, stride=LAT), :]
    lat_hi[...] = st[pl.ds(2 * LAT - 1, LON, stride=LAT), :]
    for c in w_copies:
        c.wait()

    @pl.when(scal_s[0, LON - 1] >= FIRST * TILE)
    def _():
        tend[...] = closure_tile(packed[:TILE, :], w_in, w_hid, w_out, ha, hb)


def tiles_of(packed, tend, weights, hidden, first, end):
    def tile(t, carry):
        r = pl.multiple_of(t * TILE, TILE)
        tend[pl.ds(r, TILE), :] = closure_tile(packed[pl.ds(r, TILE), :], *weights, *hidden)
        return carry

    lax.fori_loop(first, end, tile, 0)


def middle_kernel(packed, tend_f, scal, w_in, w_hid, w_out, tend, ha, hb, scal_s, sem_s):
    scal_copy = pltpu.make_async_copy(scal, scal_s, sem_s)
    scal_copy.start()
    tend[...] = jnp.zeros_like(tend)
    scal_copy.wait()
    inner_n = scal_s[0, LON - 1]
    busy = inner_n >= FIRST * TILE

    @pl.when(busy)
    def _():
        tend[:TILE, :] = tend_f[...]

    end = jnp.minimum(lax.div(inner_n, TILE), FIRST)
    tiles_of(packed, tend, (w_in, w_hid, w_out), (ha, hb), jnp.where(busy, 1, 0), end)


def last_kernel(
    west, east, south, north, adv_i, packed_i, tend_i, rank_t, rank_e, scal, coef, w_in, w_hid, w_out,
    out_h, adv, packed, tend, ha, hb, scal_s, sem_s, sem,
):
    scal_copy = pltpu.make_async_copy(scal, scal_s, sem_s)
    scal_copy.start()
    packed[...] = packed_i[...]
    tend[: FIRST * TILE, :] = tend_i[...]
    tend[FIRST * TILE :, :] = jnp.zeros((ROWS - FIRST * TILE, CH), BF)
    adv[0:LAT, :] += west[...] * coef[2 * LON : 2 * LON + LAT, :]
    adv[COLS - LAT :, :] += east[...] * coef[2 * LON + LAT :, :]
    low, high = pl.ds(0, LON, stride=LAT), pl.ds(LAT - 1, LON, stride=LAT)
    place = lax.axis_index("ty")
    north_rim = jnp.where(place == lax.axis_size("ty") - 1, F32(0.0), north[...])
    south_rim = jnp.where(place == 0, F32(0.0), south[...])
    adv[high, :] = adv[high, :] + north_rim * coef[:LON, :]
    adv[low, :] = adv[low, :] + south_rim * coef[LON : 2 * LON, :]
    edge = jnp.concatenate(
        [adv[0:LAT, :], adv[COLS - LAT :, :], jnp.zeros((64, CH), F32), adv[low, :], adv[high, :]], axis=0
    ).astype(BF)
    scal_copy.wait()
    inner_n = scal_s[0, LON - 1]
    count = inner_n + scal_s[1, 0]
    aligned_e = align16(inner_n)
    hits = iota((320 + 16, EDGE), 0) == rank_e[:1, :] - aligned_e
    append(packed, mm(one_hot(hits), edge), aligned_e)

    def unpacked(q):
        turned = pltpu.roll(rank_t[...], lax.rem(LON - q * 16, LON), 1)
        parts = []
        for i in range(4):
            aligned = align16(scal_s[0, q * 16 + 4 * i])
            cols = [jnp.broadcast_to(turned[:, 4 * i + j : 4 * i + j + 1], (LAT, 256)) for j in range(4)]
            hit = one_hot(jnp.concatenate(cols, axis=0) == iota((UGRP, 256), 1) + aligned)
            parts.append(mm(hit, tend[pl.ds(aligned, 256), :]))
        r = pl.multiple_of(q * 4 * UGRP, 4 * UGRP)
        adv[pl.ds(r, 4 * UGRP), :] += jnp.concatenate(parts, axis=0)

    done = jnp.minimum(lax.div(inner_n, TILE), FIRST)
    last = lax.div(count + TILE - 1, TILE)
    early = (last > done) & (scal_s[0, EARLY * 16] <= done * TILE)
    weights, hidden = (w_in, w_hid, w_out), (ha, hb)
    tiles_of(packed, tend, weights, hidden, done, jnp.where(early, last - 1, last))

    @pl.when(early)
    def _():
        r = pl.multiple_of((last - 1) * TILE, TILE)
        beside = [functools.partial(unpacked, q) for q in range(EARLY)]
        tend[pl.ds(r, TILE), :] = closure_tile(packed[pl.ds(r, TILE), :], *weights, *hidden, beside)

    rank_col = jnp.concatenate(
        [jnp.transpose(jnp.broadcast_to(rank_e[:1, k * 128 : k * 128 + 128], (128, 128))) for k in range(3)], axis=0
    )
    picks = jnp.concatenate([rank_col - aligned_e - 128 * k for k in range(3)], axis=1) == (
        iota((EDGE, EDGE), 1) & 127
    )
    back = mm(one_hot(picks), tend[pl.ds(aligned_e, EDGE), :])
    adv[0:LAT, :] += back[0:LAT]
    adv[COLS - LAT :, :] += back[LAT : 2 * LAT]
    adv[low, :] = adv[low, :] + back[128:256]
    adv[high, :] = adv[high, :] + back[256:384]

    def out_copy(k):
        part = pl.ds(k * (COLS // 8), COLS // 8)
        return pltpu.make_async_copy(adv.at[part], out_h.at[part], sem.at[k])

    def unpack(q, carry):
        @pl.when(jnp.logical_not(early) | (q >= EARLY))
        def _():
            unpacked(q)

        out_copy(q).start()
        return carry

    lax.fori_loop(0, 8, unpack, 0)
    for k in range(8):
        out_copy(k).wait()


ANY = pl.BlockSpec(memory_space=pl.ANY)
HBM = pl.BlockSpec(memory_space=pltpu.HBM)
VM = pl.BlockSpec(memory_space=pltpu.VMEM)


def in_hbm(x):
    return pltpu.with_memory_space_constraint(x, pltpu.HBM)


def params():
    return pltpu.CompilerParams(vmem_limit_bytes=24 << 20)


def cost(gflops):
    return pl.CostEstimate(flops=gflops * 10**9, bytes_accessed=1 << 20, transcendentals=1 << 20)


def local(state, courant, diffusion, conv_mask, w_in, w_hidden, w_out):
    n_tx, n_ty = lax.axis_size("tx"), lax.axis_size("ty")
    ring = [(i, (i + 1) % n_tx) for i in range(n_tx)]
    line = [(i, (i + 1) % n_ty) for i in range(n_ty)]
    kept = (
        ((COLS, CH), F32),
        ((ROWS, CH), BF),
        ((TILE, CH), BF),
        ((LAT, LON), I32),
        ((8, EDGE), I32),
        ((8, LON), I32),
        ((2 * LON + 2 * LAT, CH), F32),
        ((CH, HID), BF),
        ((3, HID, HID), BF),
        ((HID, CH), BF),
        ((LAT, CH), F32),
        ((LAT, CH), F32),
        ((LON, CH), F32),
        ((LON, CH), F32),
    )
    hidden = [pltpu.VMEM((TILE, HID), BF)] * 2
    smem = [pltpu.SMEM((8, LON), I32)]
    held = pl.pallas_call(
        first_kernel,
        out_shape=[pltpu.VMEM(s, t) for s, t in kept],
        in_specs=[HBM] * 7,
        out_specs=[VM] * len(kept),
        scratch_shapes=[
            pltpu.VMEM((COLS + 2 * LAT + 8, CH), F32),
            pltpu.VMEM((COLS, CH), BF),
            pltpu.VMEM((COLS, CH), BF),
            pltpu.VMEM((LAT, LON), F32),
            pltpu.VMEM((LON, LON), F32),
            pltpu.VMEM((LAT, LON), I32),
            pltpu.VMEM((LON, LON), F32),
            pltpu.VMEM((COLS // PGRP, PGRP), I32),
            *hidden,
            *smem,
            pltpu.SemaphoreType.DMA((13,)),
            pltpu.SemaphoreType.DMA,
        ],
        compiler_params=params(),
        cost_estimate=cost(1),
        name="advance_pack",
    )(*map(in_hbm, (state.reshape(COLS, CH), courant.reshape(COLS, CH), diffusion.T, conv_mask.T, w_in, w_hidden, w_out)))
    adv, packed, tend_f, rank_t, rank_e, scal, coef, w_in, w_hid, w_out, lon_lo, lon_hi, lat_lo, lat_hi = held
    west = lax.ppermute(lon_hi, "tx", ring)
    east = lax.ppermute(lon_lo, "tx", [(j, i) for i, j in ring])
    south = lax.ppermute(lat_hi, "ty", line)
    north = lax.ppermute(lat_lo, "ty", [(j, i) for i, j in line])
    tend = pl.pallas_call(
        middle_kernel,
        out_shape=pltpu.VMEM((FIRST * TILE, CH), BF),
        in_specs=[VM] * 6,
        out_specs=VM,
        scratch_shapes=[*hidden, *smem, pltpu.SemaphoreType.DMA],
        compiler_params=params(),
        cost_estimate=cost(12),
        name="closure_middle",
    )(packed, tend_f, scal, w_in, w_hid, w_out)
    out, _ = pl.pallas_call(
        last_kernel,
        out_shape=[jax.ShapeDtypeStruct((COLS, CH), F32), pltpu.VMEM((COLS, CH), F32)],
        in_specs=[VM] * 14,
        out_specs=[HBM, VM],
        input_output_aliases={4: 1},
        scratch_shapes=[
            pltpu.VMEM((ROWS, CH), BF),
            pltpu.VMEM((ROWS, CH), BF),
            *hidden,
            *smem,
            pltpu.SemaphoreType.DMA,
            pltpu.SemaphoreType.DMA((8,)),
        ],
        compiler_params=params(),
        cost_estimate=cost(4),
        name="closure_unpack",
    )(west, east, south, north, adv, packed, tend, rank_t, rank_e, scal, coef, w_in, w_hid, w_out)
    return out.reshape(LON, LAT, CH)


def solution(mesh):
    tile = P(("member", "tx"), "ty", None)
    flat = P(("member", "tx"), "ty")
    return jax.shard_map(
        local,
        mesh=mesh,
        in_specs=(tile, tile, flat, flat, P(), P(), P()),
        out_specs=tile,
        check_vma=False,
    )
```

```python
import functools

import jax
import jax.numpy as jnp
from jax import lax
from jax.experimental import pallas as pl
from jax.experimental.pallas import tpu as pltpu
from jax.sharding import PartitionSpec as P

LON, LAT, CH, HID = 128, 32, 128, 1024
COLS = LON * LAT
TILE = 512
CAP = 2048
ROWS = CAP + TILE
PGRP = 256
UGRP = 128
EDGE = 384
EARLY = 6
UNIT = 256
BF, F32, I32 = jnp.bfloat16, jnp.float32, jnp.int32


def iota(shape, dim):
    return lax.broadcasted_iota(I32, shape, dim)


def one_hot(hit):
    return jnp.where(hit, F32(1.0), F32(0.0)).astype(BF)


def mm(a, b):
    return jnp.dot(a, b, preferred_element_type=F32)


def silu(v):
    half = 0.5 * v
    return (half + half * jnp.tanh(half)).astype(BF)


def closure_tile(x, w_in, w_hid, w_out, ha, hb, beside=()):
    step = 256
    beside = list(beside)
    ha, hb = ha.at[: x.shape[0]], hb.at[: x.shape[0]]

    def layer(src, weight, dst, side):
        for n in range(0, HID, step):
            dst[:, n : n + step] = silu(mm(src, weight(n)))
            if side and n in (0, 512) and beside:
                beside.pop(0)()

    layer(x, lambda n: w_in[:, n : n + step], ha, False)
    layer(ha[...], lambda n: w_hid[0, :, n : n + step], hb, True)
    layer(hb[...], lambda n: w_hid[1, :, n : n + step], ha, True)
    layer(ha[...], lambda n: w_hid[2, :, n : n + step], hb, True)
    return mm(hb[...], w_out[...]).astype(BF)


def append(packed, rows, aligned):
    n = rows.shape[0]
    head = packed[pl.ds(aligned, 16), :].astype(F32) + rows[:16]
    packed[pl.ds(aligned, 16), :] = head.astype(BF)
    packed[pl.ds(pl.multiple_of(aligned + 16, 16), n - 16), :] = rows[16:].astype(BF)


def align16(x):
    return pl.multiple_of((x // 16) * 16, 16)


def first_kernel(
    state_h, courant_h, diff_h, mask_h, win_h, whid_h, wout_h,
    adv, packed, tend, rank_t, rank_e, scal, coef, w_in, w_hid, w_out, lon_lo, lon_hi, lat_lo, lat_hi,
    st, cou, feat, dif, dif_n, msk, rank_n, rank_r, ha, hb, scal_v, sem, sem_s,
):
    quarter = COLS // 4

    def in_copies(k):
        return (
            pltpu.make_async_copy(state_h.at[pl.ds(k * quarter, quarter)], st.at[pl.ds(k * quarter + LAT, quarter)], sem.at[k]),
            pltpu.make_async_copy(courant_h.at[pl.ds(k * quarter, quarter)], cou.at[pl.ds(k * quarter, quarter)], sem.at[4 + k]),
        )

    mask_copy = pltpu.make_async_copy(mask_h, msk, sem.at[8])
    diff_copy = pltpu.make_async_copy(diff_h, dif, sem.at[9])
    w_copies = (
        pltpu.make_async_copy(win_h, w_in, sem.at[10]),
        pltpu.make_async_copy(whid_h, w_hid, sem.at[11]),
        pltpu.make_async_copy(wout_h, w_out, sem.at[12]),
    )
    mask_copy.start()
    diff_copy.start()
    for k in range(4):
        for c in in_copies(k):
            c.start()
    for c in w_copies:
        c.start()
    packed[...] = jnp.zeros_like(packed)
    st[0:LAT, :] = jnp.zeros((LAT, CH), F32)
    st[COLS + LAT : COLS + 2 * LAT, :] = jnp.zeros((LAT, CH), F32)

    def wait_quarter(k):
        for c in in_copies(k):
            c.wait()

    mask_copy.wait()
    diff_copy.wait()
    wait_quarter(0)
    wait_quarter(1)
    dif_1 = dif[...].astype(BF).astype(F32)
    dif_2 = (dif[...] - dif_1).astype(BF).astype(F32)
    dif_3 = dif[...] - dif_1 - dif_2
    dif_n[...] = jnp.transpose(jnp.concatenate([dif_1, dif_2, dif_3, jnp.zeros((LAT, LON), F32)], axis=0))

    lat_of = iota((LAT, CH), 0)
    low = iota((LAT, CH), 1) < 64
    own_lat = (iota((LAT, CH), 1) & 31) == lat_of
    ones = jnp.ones((CH, CH), BF)

    def stencil(i):
        spread = [jnp.where(own_lat, dif_n[pl.ds(i * 16 + j, 1), :], F32(0.0)) for j in range(16)]
        d_all = mm(jnp.concatenate(spread, axis=0).astype(BF), ones)
        for j in range(16):
            r = pl.multiple_of(i * 2 * PGRP + j * LAT, LAT)
            center = st[pl.ds(r + LAT, LAT), :]
            east = st[pl.ds(r + 2 * LAT, LAT), :]
            west = st[pl.ds(r, LAT), :]
            north = jnp.where(lat_of == LAT - 1, F32(0.0), st[pl.ds(r + LAT + 1, LAT), :])
            south = jnp.where(lat_of == 0, F32(0.0), st[pl.ds(r + LAT - 1, LAT), :])
            wind = 0.5 * cou[pl.ds(r, LAT), :].astype(F32)
            turned = pltpu.roll(wind, 64, 1)
            along_lon = jnp.where(low, wind, turned)
            along_lat = jnp.where(low, turned, wind)
            d = d_all[j * LAT : (j + 1) * LAT]
            laplace = east + west + north + south - 4.0 * center
            new = center - along_lon * (east - west) - along_lat * (north - south) + d * laplace
            adv[pl.ds(r, LAT), :] = new
            feat[pl.ds(r, LAT), :] = new.astype(BF)
            coef[pl.ds(i * 16 + j, 1), :] = (d - along_lat)[LAT - 1 :]
            coef[pl.ds(LON + i * 16 + j, 1), :] = (d + along_lat)[:1]
            if isinstance(i, int) and i == 0 and j == 0:
                coef[2 * LON : 2 * LON + LAT, :] = d + along_lon
            if isinstance(i, int) and i == 7 and j == 15:
                coef[2 * LON + LAT : 2 * LON + 2 * LAT, :] = d - along_lon

    lat, lon = iota((LAT, LON), 0), iota((LAT, LON), 1)
    flags = msk[...]
    inner = (lon > 0) & (lon < LON - 1) & (lat > 0) & (lat < LAT - 1) & (flags == 1)
    inner_b = one_hot(inner)
    in_row = mm(one_hot(iota((LAT, LAT), 1) < iota((LAT, LAT), 0)), inner_b)
    per_lon = mm(jnp.ones((LAT, LAT), BF), inner_b).astype(BF)
    row_start = mm(per_lon, one_hot(iota((LON, LON), 0) < iota((LON, LON), 1)))
    rank = jnp.where(inner, in_row + row_start, F32(-4096.0))
    rank_t[...] = rank.astype(I32)
    starts = row_start[:1]
    flags_f = flags.astype(F32)
    lane = iota((1, LON), 1)
    ends = (lane == 0) | (lane == LON - 1)
    both = jnp.concatenate([rank, flags_f, jnp.zeros((LON - 2 * LAT, LON), F32)], axis=0)
    rank_n[...] = jnp.transpose(both)
    edge_row = jnp.concatenate(
        [
            rank_n[0:1, LAT : 2 * LAT],
            rank_n[LON - 1 :, LAT : 2 * LAT],
            jnp.zeros((1, 64), F32),
            jnp.where(ends, F32(0.0), flags_f[:1]),
            jnp.where(ends, F32(0.0), flags_f[LAT - 1 :]),
        ],
        axis=1,
    )
    edge_n = jnp.broadcast_to(jnp.sum(edge_row, axis=1, keepdims=True), (1, LON))
    stencil(0)
    scal_v[...] = jnp.where(iota((8, LON), 0) == 0, starts, edge_n).astype(I32)
    scal_copy = pltpu.make_async_copy(scal_v, scal, sem_s)
    scal_copy.start()
    rank_r[...] = jnp.concatenate(
        [rank_n[pl.ds(j, COLS // PGRP, stride=PGRP // LAT), :LAT] for j in range(PGRP // LAT)], axis=1
    ).astype(I32)
    edge_b = jnp.broadcast_to(edge_row, (16, EDGE)).astype(BF)
    edge_rank = mm(edge_b, one_hot(iota((EDGE, EDGE), 0) < iota((EDGE, EDGE), 1)))[:8]
    rank_e[...] = jnp.where(edge_row == 1.0, edge_rank + starts[:, LON - 1 :], F32(-4096.0)).astype(I32)
    def pack(i):
        todo = []
        for k in range(2):
            g = i * 2 + k
            aligned = align16(scal[0, g * 8])
            hits = iota((PGRP + 16, PGRP), 0) == rank_r[pl.ds(g, 1), :] - aligned
            todo.append((aligned, mm(one_hot(hits), feat[pl.ds(pl.multiple_of(g * PGRP, PGRP), PGRP), :])))
        for aligned, rows in todo:
            append(packed, rows, aligned)

    scal_copy.wait()

    def both_steps(i, carry):
        @pl.when((lax.rem(i, 2) == 1) & (i > 1))
        def _():
            wait_quarter(lax.div(i, 2) + 1)

        stencil(i)
        pack(i - 1)
        return carry

    lax.fori_loop(1, 7, both_steps, 0)
    stencil(7)
    pack(6)
    pack(7)
    lon_lo[...] = st[LAT : 2 * LAT, :]
    lon_hi[...] = st[COLS : COLS + LAT, :]
    lat_lo[...] = st[pl.ds(LAT, LON, stride=LAT), :]
    lat_hi[...] = st[pl.ds(2 * LAT - 1, LON, stride=LAT), :]
    for c in w_copies:
        c.wait()

    before, _, _ = plan(scal)
    weights, hidden = (w_in, w_hid, w_out), (ha, hb)

    @pl.when(before == 2)
    def _():
        tend[...] = closure_tile(packed[:TILE, :], *weights, *hidden)

    @pl.when(before == 1)
    def _():
        tend[:UNIT, :] = closure_tile(packed[:UNIT, :], *weights, *hidden)


def closure_units(packed, tend, weights, hidden, first, end):
    def rows(unit, size):
        part = pl.ds(pl.multiple_of(unit * UNIT, UNIT), size)
        tend[part, :] = closure_tile(packed[part, :], *weights, *hidden)

    odd = lax.rem(end - first, 2)

    @pl.when(odd == 1)
    def _():
        rows(first, UNIT)

    def tile(t, carry):
        rows(first + odd + 2 * t, TILE)
        return carry

    lax.fori_loop(0, lax.div(end - first, 2), tile, 0)


def plan(scal):
    inner_n = scal[0, LON - 1]
    count = inner_n + scal[1, 0]
    total = lax.div(count + UNIT - 1, UNIT)
    before = jnp.where(count >= 1536, 2, jnp.where(count >= 1280, 1, 0))
    inner = lax.div(inner_n, UNIT)
    less = (inner > before) & (lax.rem(inner - before, 2) == 1) & (total - inner < 2)
    return before, jnp.where(less, inner - 1, inner), total


def middle_kernel(packed, tend_f, scal, w_in, w_hid, w_out, tend, ha, hb):
    tend[...] = jnp.zeros_like(tend)
    before, inner, _ = plan(scal)

    @pl.when(before >= 1)
    def _():
        tend[:UNIT, :] = tend_f[:UNIT, :]

    @pl.when(before == 2)
    def _():
        tend[UNIT:TILE, :] = tend_f[UNIT:, :]

    closure_units(packed, tend, (w_in, w_hid, w_out), (ha, hb), before, inner)


def last_kernel(
    west, east, south, north, adv_i, packed_i, tend_i, rank_t, rank_e, scal, coef, w_in, w_hid, w_out,
    out_h, adv, packed, tend, ha, hb, sem,
):
    adv[0:LAT, :] += west[...] * coef[2 * LON : 2 * LON + LAT, :]
    adv[COLS - LAT :, :] += east[...] * coef[2 * LON + LAT :, :]
    low, high = pl.ds(0, LON, stride=LAT), pl.ds(LAT - 1, LON, stride=LAT)
    place = lax.axis_index("ty")
    north_rim = jnp.where(place == lax.axis_size("ty") - 1, F32(0.0), north[...])
    south_rim = jnp.where(place == 0, F32(0.0), south[...])
    adv[high, :] = adv[high, :] + north_rim * coef[:LON, :]
    adv[low, :] = adv[low, :] + south_rim * coef[LON : 2 * LON, :]
    edge = jnp.concatenate(
        [adv[0:LAT, :], adv[COLS - LAT :, :], jnp.zeros((64, CH), F32), adv[low, :], adv[high, :]], axis=0
    ).astype(BF)
    inner_n = scal[0, LON - 1]
    aligned_e = align16(inner_n)
    hits = iota((320 + 16, EDGE), 0) == rank_e[:1, :] - aligned_e
    append(packed, mm(one_hot(hits), edge), aligned_e)

    def unpacked(q):
        turned = pltpu.roll(rank_t[...], lax.rem(LON - q * 16, LON), 1)
        parts = []
        for i in range(4):
            aligned = align16(scal[0, q * 16 + 4 * i])
            cols = [jnp.broadcast_to(turned[:, 4 * i + j : 4 * i + j + 1], (LAT, 256)) for j in range(4)]
            hit = one_hot(jnp.concatenate(cols, axis=0) == iota((UGRP, 256), 1) + aligned)
            parts.append(mm(hit, tend[pl.ds(aligned, 256), :]))
        r = pl.multiple_of(q * 4 * UGRP, 4 * UGRP)
        adv[pl.ds(r, 4 * UGRP), :] += jnp.concatenate(parts, axis=0)

    _, done, total = plan(scal)
    early = (total - done >= 2) & (scal[0, EARLY * 16] <= (total - 2) * UNIT)
    weights, hidden = (w_in, w_hid, w_out), (ha, hb)
    closure_units(packed, tend, weights, hidden, done, jnp.where(early, total - 2, total))

    @pl.when(early)
    def _():
        part = pl.ds(pl.multiple_of((total - 2) * UNIT, UNIT), TILE)
        beside = [functools.partial(unpacked, q) for q in range(EARLY)]
        tend[part, :] = closure_tile(packed[part, :], *weights, *hidden, beside)

    rank_col = jnp.concatenate(
        [jnp.transpose(jnp.broadcast_to(rank_e[:1, k * 128 : k * 128 + 128], (128, 128))) for k in range(3)], axis=0
    )
    picks = jnp.concatenate([rank_col - aligned_e - 128 * k for k in range(3)], axis=1) == (
        iota((EDGE, EDGE), 1) & 127
    )
    back = mm(one_hot(picks), tend[pl.ds(aligned_e, EDGE), :])
    adv[0:LAT, :] += back[0:LAT]
    adv[COLS - LAT :, :] += back[LAT : 2 * LAT]
    adv[low, :] = adv[low, :] + back[128:256]
    adv[high, :] = adv[high, :] + back[256:384]

    def out_copy(k):
        part = pl.ds(k * (COLS // 8), COLS // 8)
        return pltpu.make_async_copy(adv.at[part], out_h.at[part], sem.at[k])

    def unpack(q, carry):
        @pl.when(jnp.logical_not(early) | (q >= EARLY))
        def _():
            unpacked(q)

        out_copy(q).start()
        return carry

    lax.fori_loop(0, 8, unpack, 0)
    for k in range(8):
        out_copy(k).wait()


ANY = pl.BlockSpec(memory_space=pl.ANY)
HBM = pl.BlockSpec(memory_space=pltpu.HBM)
VM = pl.BlockSpec(memory_space=pltpu.VMEM)
SM = pl.BlockSpec(memory_space=pltpu.SMEM)


def in_hbm(x):
    return pltpu.with_memory_space_constraint(x, pltpu.HBM)


def params():
    return pltpu.CompilerParams(vmem_limit_bytes=24 << 20)


def cost(gflops):
    return pl.CostEstimate(flops=gflops * 10**9, bytes_accessed=1 << 20, transcendentals=1 << 20)


def local(state, courant, diffusion, conv_mask, w_in, w_hidden, w_out):
    n_tx, n_ty = lax.axis_size("tx"), lax.axis_size("ty")
    ring = [(i, (i + 1) % n_tx) for i in range(n_tx)]
    line = [(i, (i + 1) % n_ty) for i in range(n_ty)]
    kept = (
        ((COLS, CH), F32),
        ((ROWS, CH), BF),
        ((TILE, CH), BF),
        ((LAT, LON), I32),
        ((8, EDGE), I32),
        None,
        ((2 * LON + 2 * LAT, CH), F32),
        ((CH, HID), BF),
        ((3, HID, HID), BF),
        ((HID, CH), BF),
        ((LAT, CH), F32),
        ((LAT, CH), F32),
        ((LON, CH), F32),
        ((LON, CH), F32),
    )
    hidden = [pltpu.VMEM((TILE, HID), BF)] * 2
    held = pl.pallas_call(
        first_kernel,
        out_shape=[pltpu.VMEM(*k) if k else pltpu.SMEM((8, LON), I32) for k in kept],
        in_specs=[HBM] * 7,
        out_specs=[VM if k else SM for k in kept],
        scratch_shapes=[
            pltpu.VMEM((COLS + 2 * LAT + 8, CH), F32),
            pltpu.VMEM((COLS, CH), BF),
            pltpu.VMEM((COLS, CH), BF),
            pltpu.VMEM((LAT, LON), F32),
            pltpu.VMEM((LON, LON), F32),
            pltpu.VMEM((LAT, LON), I32),
            pltpu.VMEM((LON, LON), F32),
            pltpu.VMEM((COLS // PGRP, PGRP), I32),
            *hidden,
            pltpu.VMEM((8, LON), I32),
            pltpu.SemaphoreType.DMA((13,)),
            pltpu.SemaphoreType.DMA,
        ],
        compiler_params=params(),
        cost_estimate=cost(1),
        name="advance_pack",
    )(*map(in_hbm, (state.reshape(COLS, CH), courant.reshape(COLS, CH), diffusion.T, conv_mask.T, w_in, w_hidden, w_out)))
    adv, packed, tend_f, rank_t, rank_e, scal, coef, w_in, w_hid, w_out, lon_lo, lon_hi, lat_lo, lat_hi = held
    west = lax.ppermute(lon_hi, "tx", ring)
    east = lax.ppermute(lon_lo, "tx", [(j, i) for i, j in ring])
    south = lax.ppermute(lat_hi, "ty", line)
    north = lax.ppermute(lat_lo, "ty", [(j, i) for i, j in line])
    tend = pl.pallas_call(
        middle_kernel,
        out_shape=pltpu.VMEM((ROWS, CH), BF),
        in_specs=[VM, VM, SM, VM, VM, VM],
        out_specs=VM,
        scratch_shapes=hidden,
        compiler_params=params(),
        cost_estimate=cost(12),
        name="closure_middle",
    )(packed, tend_f, scal, w_in, w_hid, w_out)
    out, *_ = pl.pallas_call(
        last_kernel,
        out_shape=[
            jax.ShapeDtypeStruct((COLS, CH), F32),
            pltpu.VMEM((COLS, CH), F32),
            pltpu.VMEM((ROWS, CH), BF),
            pltpu.VMEM((ROWS, CH), BF),
        ],
        in_specs=[VM] * 9 + [SM] + [VM] * 4,
        out_specs=[HBM, VM, VM, VM],
        input_output_aliases={4: 1, 5: 2, 6: 3},
        scratch_shapes=[*hidden, pltpu.SemaphoreType.DMA((8,))],
        compiler_params=params(),
        cost_estimate=cost(4),
        name="closure_unpack",
    )(west, east, south, north, adv, packed, tend, rank_t, rank_e, scal, coef, w_in, w_hid, w_out)
    return out.reshape(LON, LAT, CH)


def solution(mesh):
    tile = P(("member", "tx"), "ty", None)
    flat = P(("member", "tx"), "ty")
    return jax.shard_map(
        local,
        mesh=mesh,
        in_specs=(tile, tile, flat, flat, P(), P(), P()),
        out_specs=tile,
        check_vma=False,
    )
```

```python
import functools

import jax
import jax.numpy as jnp
from jax import lax
from jax.experimental import pallas as pl
from jax.experimental.pallas import tpu as pltpu
from jax.sharding import PartitionSpec as P

LON, LAT, CH, HID = 128, 32, 128, 1024
COLS = LON * LAT
TILE = 512
CAP = 2048
ROWS = CAP + TILE
PGRP = 256
UGRP = 128
EDGE = 384
EARLY = 6
UNIT = 256
EARLY_UNITS = 4
BF, F32, I32 = jnp.bfloat16, jnp.float32, jnp.int32


def iota(shape, dim):
    return lax.broadcasted_iota(I32, shape, dim)


def one_hot(hit):
    return jnp.where(hit, F32(1.0), F32(0.0)).astype(BF)


def mm(a, b):
    return jnp.dot(a, b, preferred_element_type=F32)


def silu(v):
    half = 0.5 * v
    return (half + half * jnp.tanh(half)).astype(BF)


def closure_tile(x, w_in, w_hid, w_out, ha, hb, beside=()):
    step = 256
    beside = list(beside)
    ha, hb = ha.at[: x.shape[0]], hb.at[: x.shape[0]]

    def layer(src, weight, dst, side):
        for n in range(0, HID, step):
            dst[:, n : n + step] = silu(mm(src, weight(n)))
            if side and n in (0, 512) and beside:
                beside.pop(0)()

    layer(x, lambda n: w_in[:, n : n + step], ha, False)
    layer(ha[...], lambda n: w_hid[0, :, n : n + step], hb, True)
    layer(hb[...], lambda n: w_hid[1, :, n : n + step], ha, True)
    layer(ha[...], lambda n: w_hid[2, :, n : n + step], hb, True)
    return mm(hb[...], w_out[...]).astype(BF)


def append(packed, rows, aligned):
    n = rows.shape[0]
    head = packed[pl.ds(aligned, 16), :].astype(F32) + rows[:16]
    packed[pl.ds(aligned, 16), :] = head.astype(BF)
    packed[pl.ds(pl.multiple_of(aligned + 16, 16), n - 16), :] = rows[16:].astype(BF)


def align16(x):
    return pl.multiple_of((x // 16) * 16, 16)


def first_kernel(
    state_h, courant_h, diff_h, mask_h, win_h, whid_h, wout_h,
    adv, packed, tend, rank_t, rank_e, scal, coef, w_in, w_hid, w_out, lon_lo, lon_hi, lat_lo, lat_hi,
    st, cou, feat, dif, dif_n, msk, rank_n, rank_r, ha, hb, scal_v, sem, sem_s,
):
    quarter = COLS // 4

    def in_copies(k):
        return (
            pltpu.make_async_copy(state_h.at[pl.ds(k * quarter, quarter)], st.at[pl.ds(k * quarter + LAT, quarter)], sem.at[k]),
            pltpu.make_async_copy(courant_h.at[pl.ds(k * quarter, quarter)], cou.at[pl.ds(k * quarter, quarter)], sem.at[4 + k]),
        )

    mask_copy = pltpu.make_async_copy(mask_h, msk, sem.at[8])
    diff_copy = pltpu.make_async_copy(diff_h, dif, sem.at[9])
    w_copies = (
        pltpu.make_async_copy(win_h, w_in, sem.at[10]),
        pltpu.make_async_copy(whid_h, w_hid, sem.at[11]),
        pltpu.make_async_copy(wout_h, w_out, sem.at[12]),
    )
    mask_copy.start()
    diff_copy.start()
    for k in range(4):
        for c in in_copies(k):
            c.start()
    for c in w_copies:
        c.start()
    packed[...] = jnp.zeros_like(packed)
    tend[...] = jnp.zeros_like(tend)
    st[0:LAT, :] = jnp.zeros((LAT, CH), F32)
    st[COLS + LAT : COLS + 2 * LAT, :] = jnp.zeros((LAT, CH), F32)

    def wait_quarter(k):
        for c in in_copies(k):
            c.wait()

    mask_copy.wait()
    diff_copy.wait()
    dif_1 = dif[...].astype(BF).astype(F32)
    dif_2 = (dif[...] - dif_1).astype(BF).astype(F32)
    dif_3 = dif[...] - dif_1 - dif_2
    dif_n[...] = jnp.transpose(jnp.concatenate([dif_1, dif_2, dif_3, jnp.zeros((LAT, LON), F32)], axis=0))

    lat_of = iota((LAT, CH), 0)
    low = iota((LAT, CH), 1) < 64
    own_lat = (iota((LAT, CH), 1) & 31) == lat_of
    ones = jnp.ones((CH, CH), BF)

    def stencil(i):
        spread = [jnp.where(own_lat, dif_n[pl.ds(i * 16 + j, 1), :], F32(0.0)) for j in range(16)]
        d_all = mm(jnp.concatenate(spread, axis=0).astype(BF), ones)
        for j in range(16):
            r = pl.multiple_of(i * 2 * PGRP + j * LAT, LAT)
            center = st[pl.ds(r + LAT, LAT), :]
            east = st[pl.ds(r + 2 * LAT, LAT), :]
            west = st[pl.ds(r, LAT), :]
            north = jnp.where(lat_of == LAT - 1, F32(0.0), st[pl.ds(r + LAT + 1, LAT), :])
            south = jnp.where(lat_of == 0, F32(0.0), st[pl.ds(r + LAT - 1, LAT), :])
            wind = 0.5 * cou[pl.ds(r, LAT), :].astype(F32)
            turned = pltpu.roll(wind, 64, 1)
            along_lon = jnp.where(low, wind, turned)
            along_lat = jnp.where(low, turned, wind)
            d = d_all[j * LAT : (j + 1) * LAT]
            laplace = east + west + north + south - 4.0 * center
            new = center - along_lon * (east - west) - along_lat * (north - south) + d * laplace
            adv[pl.ds(r, LAT), :] = new
            feat[pl.ds(r, LAT), :] = new.astype(BF)
            coef[pl.ds(i * 16 + j, 1), :] = (d - along_lat)[LAT - 1 :]
            coef[pl.ds(LON + i * 16 + j, 1), :] = (d + along_lat)[:1]
            if isinstance(i, int) and i == 0 and j == 0:
                coef[2 * LON : 2 * LON + LAT, :] = d + along_lon
            if isinstance(i, int) and i == 7 and j == 15:
                coef[2 * LON + LAT : 2 * LON + 2 * LAT, :] = d - along_lon

    lat, lon = iota((LAT, LON), 0), iota((LAT, LON), 1)
    flags = msk[...]
    inner = (lon > 0) & (lon < LON - 1) & (lat > 0) & (lat < LAT - 1) & (flags == 1)
    inner_b = one_hot(inner)
    in_row = mm(one_hot(iota((LAT, LAT), 1) < iota((LAT, LAT), 0)), inner_b)
    per_lon = mm(jnp.ones((LAT, LAT), BF), inner_b).astype(BF)
    row_start = mm(per_lon, one_hot(iota((LON, LON), 0) < iota((LON, LON), 1)))
    rank = jnp.where(inner, in_row + row_start, F32(-4096.0))
    rank_t[...] = rank.astype(I32)
    starts = row_start[:1]
    flags_f = flags.astype(F32)
    lane = iota((1, LON), 1)
    ends = (lane == 0) | (lane == LON - 1)
    both = jnp.concatenate([rank, flags_f, jnp.zeros((LON - 2 * LAT, LON), F32)], axis=0)
    rank_n[...] = jnp.transpose(both)
    edge_row = jnp.concatenate(
        [
            rank_n[0:1, LAT : 2 * LAT],
            rank_n[LON - 1 :, LAT : 2 * LAT],
            jnp.zeros((1, 64), F32),
            jnp.where(ends, F32(0.0), flags_f[:1]),
            jnp.where(ends, F32(0.0), flags_f[LAT - 1 :]),
        ],
        axis=1,
    )
    edge_n = jnp.broadcast_to(jnp.sum(edge_row, axis=1, keepdims=True), (1, LON))
    scal_v[...] = jnp.where(iota((8, LON), 0) == 0, starts, edge_n).astype(I32)
    scal_copy = pltpu.make_async_copy(scal_v, scal, sem_s)
    scal_copy.start()
    rank_r[...] = jnp.concatenate(
        [rank_n[pl.ds(j, COLS // PGRP, stride=PGRP // LAT), :LAT] for j in range(PGRP // LAT)], axis=1
    ).astype(I32)
    edge_b = jnp.broadcast_to(edge_row, (16, EDGE)).astype(BF)
    edge_rank = mm(edge_b, one_hot(iota((EDGE, EDGE), 0) < iota((EDGE, EDGE), 1)))[:8]
    rank_e[...] = jnp.where(edge_row == 1.0, edge_rank + starts[:, LON - 1 :], F32(-4096.0)).astype(I32)
    def pack(i):
        todo = []
        for k in range(2):
            g = i * 2 + k
            aligned = align16(scal[0, g * 8])
            hits = iota((PGRP + 16, PGRP), 0) == rank_r[pl.ds(g, 1), :] - aligned
            todo.append((aligned, mm(one_hot(hits), feat[pl.ds(pl.multiple_of(g * PGRP, PGRP), PGRP), :])))
        for aligned, rows in todo:
            append(packed, rows, aligned)

    wait_quarter(0)
    stencil(0)
    wait_quarter(1)
    scal_copy.wait()

    def both_steps(i, carry):
        @pl.when((lax.rem(i, 2) == 1) & (i > 1))
        def _():
            wait_quarter(lax.div(i, 2) + 1)

        stencil(i)
        pack(i - 1)
        return carry

    lax.fori_loop(1, 7, both_steps, 0)
    stencil(7)
    pack(6)
    pack(7)
    lon_lo[...] = st[LAT : 2 * LAT, :]
    lon_hi[...] = st[COLS : COLS + LAT, :]
    lat_lo[...] = st[pl.ds(LAT, LON, stride=LAT), :]
    lat_hi[...] = st[pl.ds(2 * LAT - 1, LON, stride=LAT), :]
    for c in w_copies:
        c.wait()

    before, _, _ = plan(scal)
    weights, hidden = (w_in, w_hid, w_out), (ha, hb)

    closure_units(packed, tend, weights, hidden, 0, before)


def closure_units(packed, tend, weights, hidden, first, end):
    def rows(unit, size):
        part = pl.ds(pl.multiple_of(unit * UNIT, UNIT), size)
        tend[part, :] = closure_tile(packed[part, :], *weights, *hidden)

    odd = lax.rem(end - first, 2)

    @pl.when(odd == 1)
    def _():
        rows(first, UNIT)

    def tile(t, carry):
        rows(first + odd + 2 * t, TILE)
        return carry

    lax.fori_loop(0, lax.div(end - first, 2), tile, 0)


def plan(scal):
    inner_n = scal[0, LON - 1]
    count = inner_n + scal[1, 0]
    total = lax.div(count + UNIT - 1, UNIT)
    load = count + jnp.where(lax.axis_index("ty") == 0, TILE, 0)
    inner = lax.div(inner_n, UNIT)
    most = jnp.where(lax.axis_index("ty") == 0, EARLY_UNITS, EARLY_UNITS - 2)
    before = jnp.minimum(jnp.clip(lax.div(load, UNIT) - 4, 0, most), inner)
    less = (inner > before) & (lax.rem(inner - before, 2) == 1) & (total - inner < 2)
    return before, jnp.where(less, inner - 1, inner), total


def middle_kernel(packed, tend_f, scal, w_in, w_hid, w_out, tend, ha, hb):
    early = EARLY_UNITS * UNIT
    tend[:early, :] = tend_f[...]
    tend[early:, :] = jnp.zeros((ROWS - early, CH), BF)
    before, inner, _ = plan(scal)
    closure_units(packed, tend, (w_in, w_hid, w_out), (ha, hb), before, inner)


def last_kernel(
    west, east, south, north, adv_i, packed_i, tend_i, rank_t, rank_e, scal, coef, w_in, w_hid, w_out,
    out_h, adv, packed, tend, ha, hb, sem,
):
    adv[0:LAT, :] += west[...] * coef[2 * LON : 2 * LON + LAT, :]
    adv[COLS - LAT :, :] += east[...] * coef[2 * LON + LAT :, :]
    low, high = pl.ds(0, LON, stride=LAT), pl.ds(LAT - 1, LON, stride=LAT)
    place = lax.axis_index("ty")
    north_rim = jnp.where(place == lax.axis_size("ty") - 1, F32(0.0), north[...])
    south_rim = jnp.where(place == 0, F32(0.0), south[...])
    adv[high, :] = adv[high, :] + north_rim * coef[:LON, :]
    adv[low, :] = adv[low, :] + south_rim * coef[LON : 2 * LON, :]
    edge = jnp.concatenate(
        [adv[0:LAT, :], adv[COLS - LAT :, :], jnp.zeros((64, CH), F32), adv[low, :], adv[high, :]], axis=0
    ).astype(BF)
    inner_n = scal[0, LON - 1]
    aligned_e = align16(inner_n)
    hits = iota((320 + 16, EDGE), 0) == rank_e[:1, :] - aligned_e
    append(packed, mm(one_hot(hits), edge), aligned_e)

    def unpacked(q):
        turned = pltpu.roll(rank_t[...], lax.rem(LON - q * 16, LON), 1)
        parts = []
        for i in range(4):
            aligned = align16(scal[0, q * 16 + 4 * i])
            cols = [jnp.broadcast_to(turned[:, 4 * i + j : 4 * i + j + 1], (LAT, 256)) for j in range(4)]
            hit = one_hot(jnp.concatenate(cols, axis=0) == iota((UGRP, 256), 1) + aligned)
            parts.append(mm(hit, tend[pl.ds(aligned, 256), :]))
        r = pl.multiple_of(q * 4 * UGRP, 4 * UGRP)
        adv[pl.ds(r, 4 * UGRP), :] += jnp.concatenate(parts, axis=0)

    _, done, total = plan(scal)
    early = (total - done >= 2) & (scal[0, EARLY * 16] <= (total - 2) * UNIT)
    weights, hidden = (w_in, w_hid, w_out), (ha, hb)
    closure_units(packed, tend, weights, hidden, done, jnp.where(early, total - 2, total))

    @pl.when(early)
    def _():
        part = pl.ds(pl.multiple_of((total - 2) * UNIT, UNIT), TILE)
        beside = [functools.partial(unpacked, q) for q in range(EARLY)]
        tend[part, :] = closure_tile(packed[part, :], *weights, *hidden, beside)

    rank_col = jnp.concatenate(
        [jnp.transpose(jnp.broadcast_to(rank_e[:1, k * 128 : k * 128 + 128], (128, 128))) for k in range(3)], axis=0
    )
    picks = jnp.concatenate([rank_col - aligned_e - 128 * k for k in range(3)], axis=1) == (
        iota((EDGE, EDGE), 1) & 127
    )
    back = mm(one_hot(picks), tend[pl.ds(aligned_e, EDGE), :])
    adv[0:LAT, :] += back[0:LAT]
    adv[COLS - LAT :, :] += back[LAT : 2 * LAT]
    adv[low, :] = adv[low, :] + back[128:256]
    adv[high, :] = adv[high, :] + back[256:384]

    def out_copy(k):
        part = pl.ds(k * (COLS // 8), COLS // 8)
        return pltpu.make_async_copy(adv.at[part], out_h.at[part], sem.at[k])

    def unpack(q, carry):
        @pl.when(jnp.logical_not(early) | (q >= EARLY))
        def _():
            unpacked(q)

        out_copy(q).start()
        return carry

    lax.fori_loop(0, 8, unpack, 0)
    for k in range(8):
        out_copy(k).wait()


ANY = pl.BlockSpec(memory_space=pl.ANY)
HBM = pl.BlockSpec(memory_space=pltpu.HBM)
VM = pl.BlockSpec(memory_space=pltpu.VMEM)
SM = pl.BlockSpec(memory_space=pltpu.SMEM)


def in_hbm(x):
    return pltpu.with_memory_space_constraint(x, pltpu.HBM)


def params():
    return pltpu.CompilerParams(vmem_limit_bytes=24 << 20)


def cost(gflops):
    return pl.CostEstimate(flops=gflops * 10**9, bytes_accessed=1 << 20, transcendentals=1 << 20)


def local(state, courant, diffusion, conv_mask, w_in, w_hidden, w_out):
    n_tx, n_ty = lax.axis_size("tx"), lax.axis_size("ty")
    ring = [(i, (i + 1) % n_tx) for i in range(n_tx)]
    line = [(i, (i + 1) % n_ty) for i in range(n_ty)]
    kept = (
        ((COLS, CH), F32),
        ((ROWS, CH), BF),
        ((EARLY_UNITS * UNIT, CH), BF),
        ((LAT, LON), I32),
        ((8, EDGE), I32),
        None,
        ((2 * LON + 2 * LAT, CH), F32),
        ((CH, HID), BF),
        ((3, HID, HID), BF),
        ((HID, CH), BF),
        ((LAT, CH), F32),
        ((LAT, CH), F32),
        ((LON, CH), F32),
        ((LON, CH), F32),
    )
    hidden = [pltpu.VMEM((TILE, HID), BF)] * 2
    held = pl.pallas_call(
        first_kernel,
        out_shape=[pltpu.VMEM(*k) if k else pltpu.SMEM((8, LON), I32) for k in kept],
        in_specs=[HBM] * 7,
        out_specs=[VM if k else SM for k in kept],
        scratch_shapes=[
            pltpu.VMEM((COLS + 2 * LAT + 8, CH), F32),
            pltpu.VMEM((COLS, CH), BF),
            pltpu.VMEM((COLS, CH), BF),
            pltpu.VMEM((LAT, LON), F32),
            pltpu.VMEM((LON, LON), F32),
            pltpu.VMEM((LAT, LON), I32),
            pltpu.VMEM((LON, LON), F32),
            pltpu.VMEM((COLS // PGRP, PGRP), I32),
            *hidden,
            pltpu.VMEM((8, LON), I32),
            pltpu.SemaphoreType.DMA((13,)),
            pltpu.SemaphoreType.DMA,
        ],
        compiler_params=params(),
        cost_estimate=cost(1),
        name="advance_pack",
    )(*map(in_hbm, (state.reshape(COLS, CH), courant.reshape(COLS, CH), diffusion.T, conv_mask.T, w_in, w_hidden, w_out)))
    adv, packed, tend_f, rank_t, rank_e, scal, coef, w_in, w_hid, w_out, lon_lo, lon_hi, lat_lo, lat_hi = held
    west = lax.ppermute(lon_hi, "tx", ring)
    east = lax.ppermute(lon_lo, "tx", [(j, i) for i, j in ring])
    south = lax.ppermute(lat_hi, "ty", line)
    north = lax.ppermute(lat_lo, "ty", [(j, i) for i, j in line])
    tend = pl.pallas_call(
        middle_kernel,
        out_shape=pltpu.VMEM((ROWS, CH), BF),
        in_specs=[VM, VM, SM, VM, VM, VM],
        out_specs=VM,
        scratch_shapes=hidden,
        compiler_params=params(),
        cost_estimate=cost(12),
        name="closure_middle",
    )(packed, tend_f, scal, w_in, w_hid, w_out)
    out, *_ = pl.pallas_call(
        last_kernel,
        out_shape=[
            jax.ShapeDtypeStruct((COLS, CH), F32),
            pltpu.VMEM((COLS, CH), F32),
            pltpu.VMEM((ROWS, CH), BF),
            pltpu.VMEM((ROWS, CH), BF),
        ],
        in_specs=[VM] * 9 + [SM] + [VM] * 4,
        out_specs=[HBM, VM, VM, VM],
        input_output_aliases={4: 1, 5: 2, 6: 3},
        scratch_shapes=[*hidden, pltpu.SemaphoreType.DMA((8,))],
        compiler_params=params(),
        cost_estimate=cost(4),
        name="closure_unpack",
    )(west, east, south, north, adv, packed, tend, rank_t, rank_e, scal, coef, w_in, w_hid, w_out)
    return out.reshape(LON, LAT, CH)


def solution(mesh):
    tile = P(("member", "tx"), "ty", None)
    flat = P(("member", "tx"), "ty")
    return jax.shard_map(
        local,
        mesh=mesh,
        in_specs=(tile, tile, flat, flat, P(), P(), P()),
        out_specs=tile,
        check_vma=False,
    )
```

```python
import functools

import jax
import jax.numpy as jnp
from jax import lax
from jax.experimental import pallas as pl
from jax.experimental.pallas import tpu as pltpu
from jax.sharding import PartitionSpec as P

LON, LAT, CH, HID = 128, 32, 128, 1024
COLS = LON * LAT
TILE = 512
CAP = 2048
ROWS = CAP + TILE
PGRP = 256
UGRP = 128
EDGE = 384
EARLY = 6
UNIT = 256
EARLY_UNITS = 4
BF, F32, I32 = jnp.bfloat16, jnp.float32, jnp.int32


def iota(shape, dim):
    return lax.broadcasted_iota(I32, shape, dim)


def one_hot(hit):
    return jnp.where(hit, F32(1.0), F32(0.0)).astype(BF)


def mm(a, b):
    return jnp.dot(a, b, preferred_element_type=F32)


def silu(v):
    half = 0.5 * v
    return (half + half * jnp.tanh(half)).astype(BF)


def closure_tile(x, w_in, w_hid, w_out, ha, hb, beside=()):
    step = 256
    beside = list(beside)
    ha, hb = ha.at[: x.shape[0]], hb.at[: x.shape[0]]

    def layer(src, weight, dst, side):
        for n in range(0, HID, step):
            dst[:, n : n + step] = silu(mm(src, weight(n)))
            if side and n in (0, 512) and beside:
                beside.pop(0)()

    layer(x, lambda n: w_in[:, n : n + step], ha, False)
    layer(ha[...], lambda n: w_hid[0, :, n : n + step], hb, True)
    layer(hb[...], lambda n: w_hid[1, :, n : n + step], ha, True)
    layer(ha[...], lambda n: w_hid[2, :, n : n + step], hb, True)
    return mm(hb[...], w_out[...]).astype(BF)


def append(packed, rows, aligned):
    n = rows.shape[0]
    head = packed[pl.ds(aligned, 16), :].astype(F32) + rows[:16]
    packed[pl.ds(aligned, 16), :] = head.astype(BF)
    packed[pl.ds(pl.multiple_of(aligned + 16, 16), n - 16), :] = rows[16:].astype(BF)


def align16(x):
    return pl.multiple_of((x // 16) * 16, 16)


def first_kernel(
    state_h, courant_h, diff_h, mask_h, win_h, whid_h, wout_h,
    adv, packed, tend, rank_t, rank_e, scal, coef, w_in, w_hid, w_out, lon_lo, lon_hi, lat_lo, lat_hi,
    st, cou, feat, dif, dif_n, msk, rank_n, rank_r, ha, hb, scal_v, sem, sem_s,
):
    quarter = COLS // 4

    def in_copies(k):
        return (
            pltpu.make_async_copy(state_h.at[pl.ds(k * quarter, quarter)], st.at[pl.ds(k * quarter + LAT, quarter)], sem.at[k]),
            pltpu.make_async_copy(courant_h.at[pl.ds(k * quarter, quarter)], cou.at[pl.ds(k * quarter, quarter)], sem.at[4 + k]),
        )

    mask_copy = pltpu.make_async_copy(mask_h, msk, sem.at[8])
    diff_copy = pltpu.make_async_copy(diff_h, dif, sem.at[9])
    w_copies = (
        pltpu.make_async_copy(win_h, w_in, sem.at[10]),
        pltpu.make_async_copy(whid_h, w_hid, sem.at[11]),
        pltpu.make_async_copy(wout_h, w_out, sem.at[12]),
    )
    mask_copy.start()
    diff_copy.start()
    for k in range(4):
        for c in in_copies(k):
            c.start()
    for c in w_copies:
        c.start()
    packed[...] = jnp.zeros_like(packed)
    tend[...] = jnp.zeros_like(tend)
    st[0:LAT, :] = jnp.zeros((LAT, CH), F32)
    st[COLS + LAT : COLS + 2 * LAT, :] = jnp.zeros((LAT, CH), F32)

    def wait_quarter(k):
        for c in in_copies(k):
            c.wait()

    mask_copy.wait()
    diff_copy.wait()
    dif_1 = dif[...].astype(BF).astype(F32)
    dif_2 = (dif[...] - dif_1).astype(BF).astype(F32)
    dif_3 = dif[...] - dif_1 - dif_2
    dif_n[...] = jnp.transpose(jnp.concatenate([dif_1, dif_2, dif_3, jnp.zeros((LAT, LON), F32)], axis=0))

    lat_of = iota((LAT, CH), 0)
    low = iota((LAT, CH), 1) < 64
    own_lat = (iota((LAT, CH), 1) & 31) == lat_of
    ones = jnp.ones((CH, CH), BF)

    def stencil(i):
        spread = [jnp.where(own_lat, dif_n[pl.ds(i * 16 + j, 1), :], F32(0.0)) for j in range(16)]
        d_all = mm(jnp.concatenate(spread, axis=0).astype(BF), ones)
        for j in range(16):
            r = pl.multiple_of(i * 2 * PGRP + j * LAT, LAT)
            center = st[pl.ds(r + LAT, LAT), :]
            east = st[pl.ds(r + 2 * LAT, LAT), :]
            west = st[pl.ds(r, LAT), :]
            north = jnp.where(lat_of == LAT - 1, F32(0.0), st[pl.ds(r + LAT + 1, LAT), :])
            south = jnp.where(lat_of == 0, F32(0.0), st[pl.ds(r + LAT - 1, LAT), :])
            wind = 0.5 * cou[pl.ds(r, LAT), :].astype(F32)
            turned = pltpu.roll(wind, 64, 1)
            along_lon = jnp.where(low, wind, turned)
            along_lat = jnp.where(low, turned, wind)
            d = d_all[j * LAT : (j + 1) * LAT]
            laplace = east + west + north + south - 4.0 * center
            new = center - along_lon * (east - west) - along_lat * (north - south) + d * laplace
            adv[pl.ds(r, LAT), :] = new
            feat[pl.ds(r, LAT), :] = new.astype(BF)
            coef[pl.ds(i * 16 + j, 1), :] = (d - along_lat)[LAT - 1 :]
            coef[pl.ds(LON + i * 16 + j, 1), :] = (d + along_lat)[:1]
            if isinstance(i, int) and i == 0 and j == 0:
                coef[2 * LON : 2 * LON + LAT, :] = d + along_lon
            if isinstance(i, int) and i == 7 and j == 15:
                coef[2 * LON + LAT : 2 * LON + 2 * LAT, :] = d - along_lon

    lat, lon = iota((LAT, LON), 0), iota((LAT, LON), 1)
    flags = msk[...]
    inner = (lon > 0) & (lon < LON - 1) & (lat > 0) & (lat < LAT - 1) & (flags == 1)
    inner_b = one_hot(inner)
    in_row = mm(one_hot(iota((LAT, LAT), 1) < iota((LAT, LAT), 0)), inner_b)
    per_lon = mm(jnp.ones((LAT, LAT), BF), inner_b).astype(BF)
    row_start = mm(per_lon, one_hot(iota((LON, LON), 0) < iota((LON, LON), 1)))
    rank = jnp.where(inner, in_row + row_start, F32(-4096.0))
    rank_t[...] = rank.astype(I32)
    starts = row_start[:1]
    flags_f = flags.astype(F32)
    lane = iota((1, LON), 1)
    ends = (lane == 0) | (lane == LON - 1)
    both = jnp.concatenate([rank, flags_f, jnp.zeros((LON - 2 * LAT, LON), F32)], axis=0)
    rank_n[...] = jnp.transpose(both)
    edge_row = jnp.concatenate(
        [
            rank_n[0:1, LAT : 2 * LAT],
            rank_n[LON - 1 :, LAT : 2 * LAT],
            jnp.zeros((1, 64), F32),
            jnp.where(ends, F32(0.0), flags_f[:1]),
            jnp.where(ends, F32(0.0), flags_f[LAT - 1 :]),
        ],
        axis=1,
    )
    edge_n = jnp.broadcast_to(jnp.sum(edge_row, axis=1, keepdims=True), (1, LON))
    scal_v[...] = jnp.where(iota((8, LON), 0) == 0, starts, edge_n).astype(I32)
    scal_copy = pltpu.make_async_copy(scal_v, scal, sem_s)
    scal_copy.start()
    rank_r[...] = jnp.concatenate(
        [rank_n[pl.ds(j, COLS // PGRP, stride=PGRP // LAT), :LAT] for j in range(PGRP // LAT)], axis=1
    ).astype(I32)
    edge_b = jnp.broadcast_to(edge_row, (16, EDGE)).astype(BF)
    edge_rank = mm(edge_b, one_hot(iota((EDGE, EDGE), 0) < iota((EDGE, EDGE), 1)))[:8]
    rank_e[...] = jnp.where(edge_row == 1.0, edge_rank + starts[:, LON - 1 :], F32(-4096.0)).astype(I32)
    def pack(i):
        todo = []
        for k in range(2):
            g = i * 2 + k
            aligned = align16(scal[0, g * 8])
            hits = iota((PGRP + 16, PGRP), 0) == rank_r[pl.ds(g, 1), :] - aligned
            todo.append((aligned, mm(one_hot(hits), feat[pl.ds(pl.multiple_of(g * PGRP, PGRP), PGRP), :])))
        for aligned, rows in todo:
            append(packed, rows, aligned)

    wait_quarter(0)
    stencil(0)
    wait_quarter(1)
    scal_copy.wait()

    def both_steps(i, carry):
        @pl.when((lax.rem(i, 2) == 1) & (i > 1))
        def _():
            wait_quarter(lax.div(i, 2) + 1)

        stencil(i)
        pack(i - 1)
        return carry

    lax.fori_loop(1, 7, both_steps, 0)
    stencil(7)
    pack(6)
    pack(7)
    lon_lo[...] = st[LAT : 2 * LAT, :]
    lon_hi[...] = st[COLS : COLS + LAT, :]
    lat_lo[...] = st[pl.ds(LAT, LON, stride=LAT), :]
    lat_hi[...] = st[pl.ds(2 * LAT - 1, LON, stride=LAT), :]
    for c in w_copies:
        c.wait()

    before, _, _ = plan(scal)
    weights, hidden = (w_in, w_hid, w_out), (ha, hb)

    closure_units(packed, tend, weights, hidden, 0, before)


def closure_units(packed, tend, weights, hidden, first, end):
    def rows(unit, size):
        part = pl.ds(pl.multiple_of(unit * UNIT, UNIT), size)
        tend[part, :] = closure_tile(packed[part, :], *weights, *hidden)

    odd = lax.rem(end - first, 2)

    @pl.when(odd == 1)
    def _():
        rows(first, UNIT)

    def tile(t, carry):
        rows(first + odd + 2 * t, TILE)
        return carry

    lax.fori_loop(0, lax.div(end - first, 2), tile, 0)


def plan(scal):
    inner_n = scal[0, LON - 1]
    count = inner_n + scal[1, 0]
    total = lax.div(count + UNIT - 1, UNIT)
    place = lax.axis_index("ty")
    more = jnp.where(place <= 1, 2, jnp.where(place <= 3, 1, 0))
    inner = lax.div(inner_n, UNIT)
    before = jnp.minimum(jnp.clip(lax.div(count, UNIT) - 4 + more, 0, EARLY_UNITS - 2 + more), inner)
    less = (inner > before) & (lax.rem(inner - before, 2) == 1) & (total - inner < 2)
    return before, jnp.where(less, inner - 1, inner), total


def middle_kernel(packed, tend_f, scal, w_in, w_hid, w_out, tend, ha, hb):
    early = EARLY_UNITS * UNIT
    tend[:early, :] = tend_f[...]
    tend[early:, :] = jnp.zeros((ROWS - early, CH), BF)
    before, inner, _ = plan(scal)
    closure_units(packed, tend, (w_in, w_hid, w_out), (ha, hb), before, inner)


def last_kernel(
    west, east, south, north, adv_i, packed_i, tend_i, rank_t, rank_e, scal, coef, w_in, w_hid, w_out,
    out_h, adv, packed, tend, ha, hb, sem,
):
    adv[0:LAT, :] += west[...] * coef[2 * LON : 2 * LON + LAT, :]
    adv[COLS - LAT :, :] += east[...] * coef[2 * LON + LAT :, :]
    low, high = pl.ds(0, LON, stride=LAT), pl.ds(LAT - 1, LON, stride=LAT)
    place = lax.axis_index("ty")
    north_rim = jnp.where(place == lax.axis_size("ty") - 1, F32(0.0), north[...])
    south_rim = jnp.where(place == 0, F32(0.0), south[...])
    adv[high, :] = adv[high, :] + north_rim * coef[:LON, :]
    adv[low, :] = adv[low, :] + south_rim * coef[LON : 2 * LON, :]
    edge = jnp.concatenate(
        [adv[0:LAT, :], adv[COLS - LAT :, :], jnp.zeros((64, CH), F32), adv[low, :], adv[high, :]], axis=0
    ).astype(BF)
    inner_n = scal[0, LON - 1]
    aligned_e = align16(inner_n)
    hits = iota((320 + 16, EDGE), 0) == rank_e[:1, :] - aligned_e
    append(packed, mm(one_hot(hits), edge), aligned_e)

    def unpacked(q):
        turned = pltpu.roll(rank_t[...], lax.rem(LON - q * 16, LON), 1)
        parts = []
        for i in range(4):
            aligned = align16(scal[0, q * 16 + 4 * i])
            cols = [jnp.broadcast_to(turned[:, 4 * i + j : 4 * i + j + 1], (LAT, 256)) for j in range(4)]
            hit = one_hot(jnp.concatenate(cols, axis=0) == iota((UGRP, 256), 1) + aligned)
            parts.append(mm(hit, tend[pl.ds(aligned, 256), :]))
        r = pl.multiple_of(q * 4 * UGRP, 4 * UGRP)
        adv[pl.ds(r, 4 * UGRP), :] += jnp.concatenate(parts, axis=0)

    _, done, total = plan(scal)
    early = (total - done >= 2) & (scal[0, EARLY * 16] <= (total - 2) * UNIT)
    weights, hidden = (w_in, w_hid, w_out), (ha, hb)
    closure_units(packed, tend, weights, hidden, done, jnp.where(early, total - 2, total))

    @pl.when(early)
    def _():
        part = pl.ds(pl.multiple_of((total - 2) * UNIT, UNIT), TILE)
        beside = [functools.partial(unpacked, q) for q in range(EARLY)]
        tend[part, :] = closure_tile(packed[part, :], *weights, *hidden, beside)

    rank_col = jnp.concatenate(
        [jnp.transpose(jnp.broadcast_to(rank_e[:1, k * 128 : k * 128 + 128], (128, 128))) for k in range(3)], axis=0
    )
    picks = jnp.concatenate([rank_col - aligned_e - 128 * k for k in range(3)], axis=1) == (
        iota((EDGE, EDGE), 1) & 127
    )
    back = mm(one_hot(picks), tend[pl.ds(aligned_e, EDGE), :])
    adv[0:LAT, :] += back[0:LAT]
    adv[COLS - LAT :, :] += back[LAT : 2 * LAT]
    adv[low, :] = adv[low, :] + back[128:256]
    adv[high, :] = adv[high, :] + back[256:384]

    def out_copy(k):
        part = pl.ds(k * (COLS // 8), COLS // 8)
        return pltpu.make_async_copy(adv.at[part], out_h.at[part], sem.at[k])

    def unpack(q, carry):
        @pl.when(jnp.logical_not(early) | (q >= EARLY))
        def _():
            unpacked(q)

        out_copy(q).start()
        return carry

    lax.fori_loop(0, 8, unpack, 0)
    for k in range(8):
        out_copy(k).wait()


ANY = pl.BlockSpec(memory_space=pl.ANY)
HBM = pl.BlockSpec(memory_space=pltpu.HBM)
VM = pl.BlockSpec(memory_space=pltpu.VMEM)
SM = pl.BlockSpec(memory_space=pltpu.SMEM)


def in_hbm(x):
    return pltpu.with_memory_space_constraint(x, pltpu.HBM)


def params():
    return pltpu.CompilerParams(vmem_limit_bytes=24 << 20)


def cost(gflops):
    return pl.CostEstimate(flops=gflops * 10**9, bytes_accessed=1 << 20, transcendentals=1 << 20)


def local(state, courant, diffusion, conv_mask, w_in, w_hidden, w_out):
    n_tx, n_ty = lax.axis_size("tx"), lax.axis_size("ty")
    ring = [(i, (i + 1) % n_tx) for i in range(n_tx)]
    line = [(i, (i + 1) % n_ty) for i in range(n_ty)]
    kept = (
        ((COLS, CH), F32),
        ((ROWS, CH), BF),
        ((EARLY_UNITS * UNIT, CH), BF),
        ((LAT, LON), I32),
        ((8, EDGE), I32),
        None,
        ((2 * LON + 2 * LAT, CH), F32),
        ((CH, HID), BF),
        ((3, HID, HID), BF),
        ((HID, CH), BF),
        ((LAT, CH), F32),
        ((LAT, CH), F32),
        ((LON, CH), F32),
        ((LON, CH), F32),
    )
    hidden = [pltpu.VMEM((TILE, HID), BF)] * 2
    held = pl.pallas_call(
        first_kernel,
        out_shape=[pltpu.VMEM(*k) if k else pltpu.SMEM((8, LON), I32) for k in kept],
        in_specs=[HBM] * 7,
        out_specs=[VM if k else SM for k in kept],
        scratch_shapes=[
            pltpu.VMEM((COLS + 2 * LAT + 8, CH), F32),
            pltpu.VMEM((COLS, CH), BF),
            pltpu.VMEM((COLS, CH), BF),
            pltpu.VMEM((LAT, LON), F32),
            pltpu.VMEM((LON, LON), F32),
            pltpu.VMEM((LAT, LON), I32),
            pltpu.VMEM((LON, LON), F32),
            pltpu.VMEM((COLS // PGRP, PGRP), I32),
            *hidden,
            pltpu.VMEM((8, LON), I32),
            pltpu.SemaphoreType.DMA((13,)),
            pltpu.SemaphoreType.DMA,
        ],
        compiler_params=params(),
        cost_estimate=cost(1),
        name="advance_pack",
    )(*map(in_hbm, (state.reshape(COLS, CH), courant.reshape(COLS, CH), diffusion.T, conv_mask.T, w_in, w_hidden, w_out)))
    adv, packed, tend_f, rank_t, rank_e, scal, coef, w_in, w_hid, w_out, lon_lo, lon_hi, lat_lo, lat_hi = held
    west = lax.ppermute(lon_hi, "tx", ring)
    east = lax.ppermute(lon_lo, "tx", [(j, i) for i, j in ring])
    south = lax.ppermute(lat_hi, "ty", line)
    north = lax.ppermute(lat_lo, "ty", [(j, i) for i, j in line])
    tend = pl.pallas_call(
        middle_kernel,
        out_shape=pltpu.VMEM((ROWS, CH), BF),
        in_specs=[VM, VM, SM, VM, VM, VM],
        out_specs=VM,
        scratch_shapes=hidden,
        compiler_params=params(),
        cost_estimate=cost(12),
        name="closure_middle",
    )(packed, tend_f, scal, w_in, w_hid, w_out)
    out, *_ = pl.pallas_call(
        last_kernel,
        out_shape=[
            jax.ShapeDtypeStruct((COLS, CH), F32),
            pltpu.VMEM((COLS, CH), F32),
            pltpu.VMEM((ROWS, CH), BF),
            pltpu.VMEM((ROWS, CH), BF),
        ],
        in_specs=[VM] * 9 + [SM] + [VM] * 4,
        out_specs=[HBM, VM, VM, VM],
        input_output_aliases={4: 1, 5: 2, 6: 3},
        scratch_shapes=[*hidden, pltpu.SemaphoreType.DMA((8,))],
        compiler_params=params(),
        cost_estimate=cost(4),
        name="closure_unpack",
    )(west, east, south, north, adv, packed, tend, rank_t, rank_e, scal, coef, w_in, w_hid, w_out)
    return out.reshape(LON, LAT, CH)


def solution(mesh):
    tile = P(("member", "tx"), "ty", None)
    flat = P(("member", "tx"), "ty")
    return jax.shard_map(
        local,
        mesh=mesh,
        in_specs=(tile, tile, flat, flat, P(), P(), P()),
        out_specs=tile,
        check_vma=False,
    )
```

```python
import functools

import jax
import jax.numpy as jnp
from jax import lax
from jax.experimental import pallas as pl
from jax.experimental.pallas import tpu as pltpu
from jax.sharding import PartitionSpec as P

LON, LAT, CH, HID = 128, 32, 128, 1024
COLS = LON * LAT
TILE = 512
CAP = 2048
ROWS = CAP + TILE
PGRP = 128
UGRP = 128
EDGE = 384
EARLY = 6
UNIT = 256
EARLY_UNITS = 4
BF, F32, I32 = jnp.bfloat16, jnp.float32, jnp.int32


def iota(shape, dim):
    return lax.broadcasted_iota(I32, shape, dim)


def one_hot(hit):
    return jnp.where(hit, F32(1.0), F32(0.0)).astype(BF)


def mm(a, b):
    return jnp.dot(a, b, preferred_element_type=F32)


def silu(v):
    half = 0.5 * v
    return (half + half * jnp.tanh(half)).astype(BF)


def closure_tile(x, w_in, w_hid, w_out, ha, hb, beside=()):
    step = 256
    beside = list(beside)
    ha, hb = ha.at[: x.shape[0]], hb.at[: x.shape[0]]

    def layer(src, weight, dst, side):
        for n in range(0, HID, step):
            dst[:, n : n + step] = silu(mm(src, weight(n)))
            if side and n in (0, 512) and beside:
                beside.pop(0)()

    layer(x, lambda n: w_in[:, n : n + step], ha, False)
    layer(ha[...], lambda n: w_hid[0, :, n : n + step], hb, True)
    layer(hb[...], lambda n: w_hid[1, :, n : n + step], ha, True)
    layer(ha[...], lambda n: w_hid[2, :, n : n + step], hb, True)
    return mm(hb[...], w_out[...]).astype(BF)


def append(packed, rows, aligned):
    n = rows.shape[0]
    head = packed[pl.ds(aligned, 16), :].astype(F32) + rows[:16]
    packed[pl.ds(aligned, 16), :] = head.astype(BF)
    packed[pl.ds(pl.multiple_of(aligned + 16, 16), n - 16), :] = rows[16:].astype(BF)


def align16(x):
    return pl.multiple_of((x // 16) * 16, 16)


def first_kernel(
    state_h, courant_h, diff_h, mask_h, win_h, whid_h, wout_h,
    adv, packed, tend, rank_t, rank_e, scal, coef, w_in, w_hid, w_out, lon_lo, lon_hi, lat_lo, lat_hi,
    st, cou, feat, dif, dif_n, msk, rank_n, rank_r, ha, hb, scal_v, sem, sem_s,
):
    quarter = COLS // 4

    def in_copies(k):
        return (
            pltpu.make_async_copy(state_h.at[pl.ds(k * quarter, quarter)], st.at[pl.ds(k * quarter + LAT, quarter)], sem.at[k]),
            pltpu.make_async_copy(courant_h.at[pl.ds(k * quarter, quarter)], cou.at[pl.ds(k * quarter, quarter)], sem.at[4 + k]),
        )

    mask_copy = pltpu.make_async_copy(mask_h, msk, sem.at[8])
    diff_copy = pltpu.make_async_copy(diff_h, dif, sem.at[9])
    w_copies = (
        pltpu.make_async_copy(win_h, w_in, sem.at[10]),
        pltpu.make_async_copy(whid_h, w_hid, sem.at[11]),
        pltpu.make_async_copy(wout_h, w_out, sem.at[12]),
    )
    mask_copy.start()
    diff_copy.start()
    for k in range(4):
        for c in in_copies(k):
            c.start()
    for c in w_copies:
        c.start()
    packed[...] = jnp.zeros_like(packed)
    tend[...] = jnp.zeros_like(tend)
    st[0:LAT, :] = jnp.zeros((LAT, CH), F32)
    st[COLS + LAT : COLS + 2 * LAT, :] = jnp.zeros((LAT, CH), F32)

    def wait_quarter(k):
        for c in in_copies(k):
            c.wait()

    mask_copy.wait()
    diff_copy.wait()
    dif_1 = dif[...].astype(BF).astype(F32)
    dif_2 = (dif[...] - dif_1).astype(BF).astype(F32)
    dif_3 = dif[...] - dif_1 - dif_2
    dif_n[...] = jnp.transpose(jnp.concatenate([dif_1, dif_2, dif_3, jnp.zeros((LAT, LON), F32)], axis=0))

    lat_of = iota((LAT, CH), 0)
    low = iota((LAT, CH), 1) < 64
    own_lat = (iota((LAT, CH), 1) & 31) == lat_of
    ones = jnp.ones((CH, CH), BF)

    def stencil(i):
        spread = [jnp.where(own_lat, dif_n[pl.ds(i * 16 + j, 1), :], F32(0.0)) for j in range(16)]
        d_all = mm(jnp.concatenate(spread, axis=0).astype(BF), ones)
        for j in range(16):
            r = pl.multiple_of(i * 4 * PGRP + j * LAT, LAT)
            center = st[pl.ds(r + LAT, LAT), :]
            east = st[pl.ds(r + 2 * LAT, LAT), :]
            west = st[pl.ds(r, LAT), :]
            north = jnp.where(lat_of == LAT - 1, F32(0.0), st[pl.ds(r + LAT + 1, LAT), :])
            south = jnp.where(lat_of == 0, F32(0.0), st[pl.ds(r + LAT - 1, LAT), :])
            wind = 0.5 * cou[pl.ds(r, LAT), :].astype(F32)
            turned = pltpu.roll(wind, 64, 1)
            along_lon = jnp.where(low, wind, turned)
            along_lat = jnp.where(low, turned, wind)
            d = d_all[j * LAT : (j + 1) * LAT]
            laplace = east + west + north + south - 4.0 * center
            new = center - along_lon * (east - west) - along_lat * (north - south) + d * laplace
            adv[pl.ds(r, LAT), :] = new
            feat[pl.ds(r, LAT), :] = new.astype(BF)
            coef[pl.ds(i * 16 + j, 1), :] = (d - along_lat)[LAT - 1 :]
            coef[pl.ds(LON + i * 16 + j, 1), :] = (d + along_lat)[:1]
            if isinstance(i, int) and i == 0 and j == 0:
                coef[2 * LON : 2 * LON + LAT, :] = d + along_lon
            if isinstance(i, int) and i == 7 and j == 15:
                coef[2 * LON + LAT : 2 * LON + 2 * LAT, :] = d - along_lon

    lat, lon = iota((LAT, LON), 0), iota((LAT, LON), 1)
    flags = msk[...]
    inner = (lon > 0) & (lon < LON - 1) & (lat > 0) & (lat < LAT - 1) & (flags == 1)
    inner_b = one_hot(inner)
    in_row = mm(one_hot(iota((LAT, LAT), 1) < iota((LAT, LAT), 0)), inner_b)
    per_lon = mm(jnp.ones((LAT, LAT), BF), inner_b).astype(BF)
    row_start = mm(per_lon, one_hot(iota((LON, LON), 0) < iota((LON, LON), 1)))
    rank = jnp.where(inner, in_row + row_start, F32(-4096.0))
    rank_t[...] = rank.astype(I32)
    starts = row_start[:1]
    flags_f = flags.astype(F32)
    lane = iota((1, LON), 1)
    ends = (lane == 0) | (lane == LON - 1)
    both = jnp.concatenate([rank, flags_f, jnp.zeros((LON - 2 * LAT, LON), F32)], axis=0)
    rank_n[...] = jnp.transpose(both)
    edge_row = jnp.concatenate(
        [
            rank_n[0:1, LAT : 2 * LAT],
            rank_n[LON - 1 :, LAT : 2 * LAT],
            jnp.zeros((1, 64), F32),
            jnp.where(ends, F32(0.0), flags_f[:1]),
            jnp.where(ends, F32(0.0), flags_f[LAT - 1 :]),
        ],
        axis=1,
    )
    edge_n = jnp.broadcast_to(jnp.sum(edge_row, axis=1, keepdims=True), (1, LON))
    scal_v[...] = jnp.where(iota((8, LON), 0) == 0, starts, edge_n).astype(I32)
    scal_copy = pltpu.make_async_copy(scal_v, scal, sem_s)
    scal_copy.start()
    rank_r[...] = jnp.concatenate(
        [rank_n[pl.ds(j, COLS // PGRP, stride=PGRP // LAT), :LAT] for j in range(PGRP // LAT)], axis=1
    ).astype(I32)
    edge_b = jnp.broadcast_to(edge_row, (16, EDGE)).astype(BF)
    edge_rank = mm(edge_b, one_hot(iota((EDGE, EDGE), 0) < iota((EDGE, EDGE), 1)))[:8]
    rank_e[...] = jnp.where(edge_row == 1.0, edge_rank + starts[:, LON - 1 :], F32(-4096.0)).astype(I32)
    def pack(i):
        todo = []
        for k in range(4):
            g = i * 4 + k
            aligned = align16(scal[0, g * 4])
            hits = iota((PGRP + 16, PGRP), 0) == rank_r[pl.ds(g, 1), :] - aligned
            todo.append((aligned, mm(one_hot(hits), feat[pl.ds(pl.multiple_of(g * PGRP, PGRP), PGRP), :])))
        for aligned, rows in todo:
            append(packed, rows, aligned)

    wait_quarter(0)
    stencil(0)
    wait_quarter(1)
    scal_copy.wait()

    def both_steps(i, carry):
        @pl.when((lax.rem(i, 2) == 1) & (i > 1))
        def _():
            wait_quarter(lax.div(i, 2) + 1)

        stencil(i)
        pack(i - 1)
        return carry

    lax.fori_loop(1, 7, both_steps, 0)
    stencil(7)
    pack(6)
    pack(7)
    lon_lo[...] = st[LAT : 2 * LAT, :]
    lon_hi[...] = st[COLS : COLS + LAT, :]
    lat_lo[...] = st[pl.ds(LAT, LON, stride=LAT), :]
    lat_hi[...] = st[pl.ds(2 * LAT - 1, LON, stride=LAT), :]
    for c in w_copies:
        c.wait()

    before, _, _ = plan(scal)
    weights, hidden = (w_in, w_hid, w_out), (ha, hb)

    closure_units(packed, tend, weights, hidden, 0, before)


def closure_units(packed, tend, weights, hidden, first, end):
    def rows(unit, size):
        part = pl.ds(pl.multiple_of(unit * UNIT, UNIT), size)
        tend[part, :] = closure_tile(packed[part, :], *weights, *hidden)

    odd = lax.rem(end - first, 2)

    @pl.when(odd == 1)
    def _():
        rows(first, UNIT)

    def tile(t, carry):
        rows(first + odd + 2 * t, TILE)
        return carry

    lax.fori_loop(0, lax.div(end - first, 2), tile, 0)


def plan(scal):
    inner_n = scal[0, LON - 1]
    count = inner_n + scal[1, 0]
    total = lax.div(count + UNIT - 1, UNIT)
    place = lax.axis_index("ty")
    more = jnp.where(place <= 1, 2, jnp.where(place <= 3, 1, 0))
    inner = lax.div(inner_n, UNIT)
    before = jnp.minimum(jnp.clip(lax.div(count, UNIT) - 4 + more, 0, EARLY_UNITS - 2 + more), inner)
    less = (inner > before) & (lax.rem(inner - before, 2) == 1) & (total - inner < 2)
    return before, jnp.where(less, inner - 1, inner), total


def middle_kernel(packed, tend_f, scal, w_in, w_hid, w_out, tend, ha, hb):
    early = EARLY_UNITS * UNIT
    tend[:early, :] = tend_f[...]
    tend[early:, :] = jnp.zeros((ROWS - early, CH), BF)
    before, inner, _ = plan(scal)
    closure_units(packed, tend, (w_in, w_hid, w_out), (ha, hb), before, inner)


def last_kernel(
    west, east, south, north, adv_i, packed_i, tend_i, rank_t, rank_e, scal, coef, w_in, w_hid, w_out,
    out_h, adv, packed, tend, ha, hb, sem,
):
    adv[0:LAT, :] += west[...] * coef[2 * LON : 2 * LON + LAT, :]
    adv[COLS - LAT :, :] += east[...] * coef[2 * LON + LAT :, :]
    low, high = pl.ds(0, LON, stride=LAT), pl.ds(LAT - 1, LON, stride=LAT)
    place = lax.axis_index("ty")
    north_rim = jnp.where(place == lax.axis_size("ty") - 1, F32(0.0), north[...])
    south_rim = jnp.where(place == 0, F32(0.0), south[...])
    adv[high, :] = adv[high, :] + north_rim * coef[:LON, :]
    adv[low, :] = adv[low, :] + south_rim * coef[LON : 2 * LON, :]
    edge = jnp.concatenate(
        [adv[0:LAT, :], adv[COLS - LAT :, :], jnp.zeros((64, CH), F32), adv[low, :], adv[high, :]], axis=0
    ).astype(BF)
    inner_n = scal[0, LON - 1]
    aligned_e = align16(inner_n)
    hits = iota((320 + 16, EDGE), 0) == rank_e[:1, :] - aligned_e
    append(packed, mm(one_hot(hits), edge), aligned_e)

    def unpacked(q):
        turned = pltpu.roll(rank_t[...], lax.rem(LON - q * 16, LON), 1)
        parts = []
        for i in range(4):
            aligned = align16(scal[0, q * 16 + 4 * i])
            cols = [jnp.broadcast_to(turned[:, 4 * i + j : 4 * i + j + 1], (LAT, 256)) for j in range(4)]
            hit = one_hot(jnp.concatenate(cols, axis=0) == iota((UGRP, 256), 1) + aligned)
            parts.append(mm(hit, tend[pl.ds(aligned, 256), :]))
        r = pl.multiple_of(q * 4 * UGRP, 4 * UGRP)
        adv[pl.ds(r, 4 * UGRP), :] += jnp.concatenate(parts, axis=0)

    _, done, total = plan(scal)
    early = (total - done >= 2) & (scal[0, EARLY * 16] <= (total - 2) * UNIT)
    weights, hidden = (w_in, w_hid, w_out), (ha, hb)
    closure_units(packed, tend, weights, hidden, done, jnp.where(early, total - 2, total))

    @pl.when(early)
    def _():
        part = pl.ds(pl.multiple_of((total - 2) * UNIT, UNIT), TILE)
        beside = [functools.partial(unpacked, q) for q in range(EARLY)]
        tend[part, :] = closure_tile(packed[part, :], *weights, *hidden, beside)

    rank_col = jnp.concatenate(
        [jnp.transpose(jnp.broadcast_to(rank_e[:1, k * 128 : k * 128 + 128], (128, 128))) for k in range(3)], axis=0
    )
    picks = jnp.concatenate([rank_col - aligned_e - 128 * k for k in range(3)], axis=1) == (
        iota((EDGE, EDGE), 1) & 127
    )
    back = mm(one_hot(picks), tend[pl.ds(aligned_e, EDGE), :])
    adv[0:LAT, :] += back[0:LAT]
    adv[COLS - LAT :, :] += back[LAT : 2 * LAT]
    adv[low, :] = adv[low, :] + back[128:256]
    adv[high, :] = adv[high, :] + back[256:384]

    def out_copy(k):
        part = pl.ds(k * (COLS // 8), COLS // 8)
        return pltpu.make_async_copy(adv.at[part], out_h.at[part], sem.at[k])

    def unpack(q, carry):
        @pl.when(jnp.logical_not(early) | (q >= EARLY))
        def _():
            unpacked(q)

        out_copy(q).start()
        return carry

    lax.fori_loop(0, 8, unpack, 0)
    for k in range(8):
        out_copy(k).wait()


ANY = pl.BlockSpec(memory_space=pl.ANY)
HBM = pl.BlockSpec(memory_space=pltpu.HBM)
VM = pl.BlockSpec(memory_space=pltpu.VMEM)
SM = pl.BlockSpec(memory_space=pltpu.SMEM)


def in_hbm(x):
    return pltpu.with_memory_space_constraint(x, pltpu.HBM)


def params():
    return pltpu.CompilerParams(vmem_limit_bytes=24 << 20)


def cost(gflops):
    return pl.CostEstimate(flops=gflops * 10**9, bytes_accessed=1 << 20, transcendentals=1 << 20)


def local(state, courant, diffusion, conv_mask, w_in, w_hidden, w_out):
    n_tx, n_ty = lax.axis_size("tx"), lax.axis_size("ty")
    ring = [(i, (i + 1) % n_tx) for i in range(n_tx)]
    line = [(i, (i + 1) % n_ty) for i in range(n_ty)]
    kept = (
        ((COLS, CH), F32),
        ((ROWS, CH), BF),
        ((EARLY_UNITS * UNIT, CH), BF),
        ((LAT, LON), I32),
        ((8, EDGE), I32),
        None,
        ((2 * LON + 2 * LAT, CH), F32),
        ((CH, HID), BF),
        ((3, HID, HID), BF),
        ((HID, CH), BF),
        ((LAT, CH), F32),
        ((LAT, CH), F32),
        ((LON, CH), F32),
        ((LON, CH), F32),
    )
    hidden = [pltpu.VMEM((TILE, HID), BF)] * 2
    held = pl.pallas_call(
        first_kernel,
        out_shape=[pltpu.VMEM(*k) if k else pltpu.SMEM((8, LON), I32) for k in kept],
        in_specs=[HBM] * 7,
        out_specs=[VM if k else SM for k in kept],
        scratch_shapes=[
            pltpu.VMEM((COLS + 2 * LAT + 8, CH), F32),
            pltpu.VMEM((COLS, CH), BF),
            pltpu.VMEM((COLS, CH), BF),
            pltpu.VMEM((LAT, LON), F32),
            pltpu.VMEM((LON, LON), F32),
            pltpu.VMEM((LAT, LON), I32),
            pltpu.VMEM((LON, LON), F32),
            pltpu.VMEM((COLS // PGRP, PGRP), I32),
            *hidden,
            pltpu.VMEM((8, LON), I32),
            pltpu.SemaphoreType.DMA((13,)),
            pltpu.SemaphoreType.DMA,
        ],
        compiler_params=params(),
        cost_estimate=cost(1),
        name="advance_pack",
    )(*map(in_hbm, (state.reshape(COLS, CH), courant.reshape(COLS, CH), diffusion.T, conv_mask.T, w_in, w_hidden, w_out)))
    adv, packed, tend_f, rank_t, rank_e, scal, coef, w_in, w_hid, w_out, lon_lo, lon_hi, lat_lo, lat_hi = held
    west = lax.ppermute(lon_hi, "tx", ring)
    east = lax.ppermute(lon_lo, "tx", [(j, i) for i, j in ring])
    south = lax.ppermute(lat_hi, "ty", line)
    north = lax.ppermute(lat_lo, "ty", [(j, i) for i, j in line])
    tend = pl.pallas_call(
        middle_kernel,
        out_shape=pltpu.VMEM((ROWS, CH), BF),
        in_specs=[VM, VM, SM, VM, VM, VM],
        out_specs=VM,
        scratch_shapes=hidden,
        compiler_params=params(),
        cost_estimate=cost(12),
        name="closure_middle",
    )(packed, tend_f, scal, w_in, w_hid, w_out)
    out, *_ = pl.pallas_call(
        last_kernel,
        out_shape=[
            jax.ShapeDtypeStruct((COLS, CH), F32),
            pltpu.VMEM((COLS, CH), F32),
            pltpu.VMEM((ROWS, CH), BF),
            pltpu.VMEM((ROWS, CH), BF),
        ],
        in_specs=[VM] * 9 + [SM] + [VM] * 4,
        out_specs=[HBM, VM, VM, VM],
        input_output_aliases={4: 1, 5: 2, 6: 3},
        scratch_shapes=[*hidden, pltpu.SemaphoreType.DMA((8,))],
        compiler_params=params(),
        cost_estimate=cost(4),
        name="closure_unpack",
    )(west, east, south, north, adv, packed, tend, rank_t, rank_e, scal, coef, w_in, w_hid, w_out)
    return out.reshape(LON, LAT, CH)


def solution(mesh):
    tile = P(("member", "tx"), "ty", None)
    flat = P(("member", "tx"), "ty")
    return jax.shard_map(
        local,
        mesh=mesh,
        in_specs=(tile, tile, flat, flat, P(), P(), P()),
        out_specs=tile,
        check_vma=False,
    )
```

```python
import functools

import jax
import jax.numpy as jnp
from jax import lax
from jax.experimental import pallas as pl
from jax.experimental.pallas import tpu as pltpu
from jax.sharding import PartitionSpec as P

LON, LAT, CH, HID = 128, 32, 128, 1024
COLS = LON * LAT
TILE = 512
CAP = 2048
ROWS = CAP + TILE
PGRP = 128
UGRP = 128
EDGE = 384
EARLY = 6
UNIT = 256
EARLY_UNITS = 4
BF, F32, I32 = jnp.bfloat16, jnp.float32, jnp.int32


def iota(shape, dim):
    return lax.broadcasted_iota(I32, shape, dim)


def one_hot(hit):
    return jnp.where(hit, F32(1.0), F32(0.0)).astype(BF)


def mm(a, b):
    return jnp.dot(a, b, preferred_element_type=F32)


def silu(v):
    half = 0.5 * v
    return (half + half * jnp.tanh(half)).astype(BF)


def closure_tile(x, w_in, w_hid, w_out, ha, hb, beside=()):
    step = 256
    beside = list(beside)
    ha, hb = ha.at[: x.shape[0]], hb.at[: x.shape[0]]

    def layer(src, weight, dst, side):
        for n in range(0, HID, step):
            dst[:, n : n + step] = silu(mm(src, weight(n)))
            if side and n in (0, 512) and beside:
                beside.pop(0)()

    layer(x, lambda n: w_in[:, n : n + step], ha, False)
    layer(ha[...], lambda n: w_hid[0, :, n : n + step], hb, True)
    layer(hb[...], lambda n: w_hid[1, :, n : n + step], ha, True)
    layer(ha[...], lambda n: w_hid[2, :, n : n + step], hb, True)
    return mm(hb[...], w_out[...]).astype(BF)


def append(packed, rows, aligned):
    n = rows.shape[0]
    head = packed[pl.ds(aligned, 16), :].astype(F32) + rows[:16]
    packed[pl.ds(aligned, 16), :] = head.astype(BF)
    packed[pl.ds(pl.multiple_of(aligned + 16, 16), n - 16), :] = rows[16:].astype(BF)


def align16(x):
    return pl.multiple_of((x // 16) * 16, 16)


def first_kernel(
    state_h, courant_h, diff_h, mask_h, win_h, whid_h, wout_h,
    adv, packed, tend, rank_t, rank_e, scal, coef, w_in, w_hid, w_out, lon_lo, lon_hi, lat_lo, lat_hi,
    st, cou, feat, dif, dif_n, msk, rank_n, rank_r, ha, hb, scal_v, sem, sem_s,
):
    quarter = COLS // 4

    def in_copies(k):
        return (
            pltpu.make_async_copy(state_h.at[pl.ds(k * quarter, quarter)], st.at[pl.ds(k * quarter + LAT, quarter)], sem.at[k]),
            pltpu.make_async_copy(courant_h.at[pl.ds(k * quarter, quarter)], cou.at[pl.ds(k * quarter, quarter)], sem.at[4 + k]),
        )

    mask_copy = pltpu.make_async_copy(mask_h, msk, sem.at[8])
    diff_copy = pltpu.make_async_copy(diff_h, dif, sem.at[9])
    w_copies = (
        pltpu.make_async_copy(win_h, w_in, sem.at[10]),
        pltpu.make_async_copy(whid_h, w_hid, sem.at[11]),
        pltpu.make_async_copy(wout_h, w_out, sem.at[12]),
    )
    mask_copy.start()
    diff_copy.start()
    for k in range(4):
        for c in in_copies(k):
            c.start()
    for c in w_copies:
        c.start()
    packed[...] = jnp.zeros_like(packed)
    tend[...] = jnp.zeros_like(tend)
    st[0:LAT, :] = jnp.zeros((LAT, CH), F32)
    st[COLS + LAT : COLS + 2 * LAT, :] = jnp.zeros((LAT, CH), F32)

    def wait_quarter(k):
        for c in in_copies(k):
            c.wait()

    mask_copy.wait()
    diff_copy.wait()
    dif_1 = dif[...].astype(BF).astype(F32)
    dif_2 = (dif[...] - dif_1).astype(BF).astype(F32)
    dif_3 = dif[...] - dif_1 - dif_2
    dif_n[...] = jnp.transpose(jnp.concatenate([dif_1, dif_2, dif_3, jnp.zeros((LAT, LON), F32)], axis=0))

    lat_of = iota((LAT, CH), 0)
    low = iota((LAT, CH), 1) < 64
    own_lat = (iota((LAT, CH), 1) & 31) == lat_of
    ones = jnp.ones((CH, CH), BF)

    def stencil(i):
        spread = [jnp.where(own_lat, dif_n[pl.ds(i * 16 + j, 1), :], F32(0.0)) for j in range(16)]
        d_all = mm(jnp.concatenate(spread, axis=0).astype(BF), ones)
        for j in range(16):
            r = pl.multiple_of(i * 4 * PGRP + j * LAT, LAT)
            center = st[pl.ds(r + LAT, LAT), :]
            east = st[pl.ds(r + 2 * LAT, LAT), :]
            west = st[pl.ds(r, LAT), :]
            north = jnp.where(lat_of == LAT - 1, F32(0.0), st[pl.ds(r + LAT + 1, LAT), :])
            south = jnp.where(lat_of == 0, F32(0.0), st[pl.ds(r + LAT - 1, LAT), :])
            wind = 0.5 * cou[pl.ds(r, LAT), :].astype(F32)
            turned = pltpu.roll(wind, 64, 1)
            along_lon = jnp.where(low, wind, turned)
            along_lat = jnp.where(low, turned, wind)
            d = d_all[j * LAT : (j + 1) * LAT]
            laplace = east + west + north + south - 4.0 * center
            new = center - along_lon * (east - west) - along_lat * (north - south) + d * laplace
            adv[pl.ds(r, LAT), :] = new
            feat[pl.ds(r, LAT), :] = new.astype(BF)
            coef[pl.ds(i * 16 + j, 1), :] = (d - along_lat)[LAT - 1 :]
            coef[pl.ds(LON + i * 16 + j, 1), :] = (d + along_lat)[:1]
            if isinstance(i, int) and i == 0 and j == 0:
                coef[2 * LON : 2 * LON + LAT, :] = d + along_lon
            if isinstance(i, int) and i == 7 and j == 15:
                coef[2 * LON + LAT : 2 * LON + 2 * LAT, :] = d - along_lon

    lat, lon = iota((LAT, LON), 0), iota((LAT, LON), 1)
    flags = msk[...]
    inner = (lon > 0) & (lon < LON - 1) & (lat > 0) & (lat < LAT - 1) & (flags == 1)
    inner_b = one_hot(inner)
    in_row = mm(one_hot(iota((LAT, LAT), 1) < iota((LAT, LAT), 0)), inner_b)
    per_lon = mm(jnp.ones((LAT, LAT), BF), inner_b).astype(BF)
    row_start = mm(per_lon, one_hot(iota((LON, LON), 0) < iota((LON, LON), 1)))
    rank = jnp.where(inner, in_row + row_start, F32(-4096.0))
    rank_t[...] = rank.astype(I32)
    starts = row_start[:1]
    flags_f = flags.astype(F32)
    lane = iota((1, LON), 1)
    ends = (lane == 0) | (lane == LON - 1)
    both = jnp.concatenate([rank, flags_f, jnp.zeros((LON - 2 * LAT, LON), F32)], axis=0)
    rank_n[...] = jnp.transpose(both)
    edge_row = jnp.concatenate(
        [
            rank_n[0:1, LAT : 2 * LAT],
            rank_n[LON - 1 :, LAT : 2 * LAT],
            jnp.zeros((1, 64), F32),
            jnp.where(ends, F32(0.0), flags_f[:1]),
            jnp.where(ends, F32(0.0), flags_f[LAT - 1 :]),
        ],
        axis=1,
    )
    edge_n = jnp.broadcast_to(jnp.sum(edge_row, axis=1, keepdims=True), (1, LON))
    scal_v[...] = jnp.where(iota((8, LON), 0) == 0, starts, edge_n).astype(I32)
    scal_copy = pltpu.make_async_copy(scal_v, scal, sem_s)
    scal_copy.start()
    rank_r[...] = jnp.concatenate(
        [rank_n[pl.ds(j, COLS // PGRP, stride=PGRP // LAT), :LAT] for j in range(PGRP // LAT)], axis=1
    ).astype(I32)
    edge_b = jnp.broadcast_to(edge_row, (16, EDGE)).astype(BF)
    edge_rank = mm(edge_b, one_hot(iota((EDGE, EDGE), 0) < iota((EDGE, EDGE), 1)))[:8]
    rank_e[...] = jnp.where(edge_row == 1.0, edge_rank + starts[:, LON - 1 :], F32(-4096.0)).astype(I32)
    def pack(i):
        todo = []
        for k in range(4):
            g = i * 4 + k
            aligned = align16(scal[0, g * 4])
            hits = iota((PGRP + 16, PGRP), 0) == rank_r[pl.ds(g, 1), :] - aligned
            todo.append((aligned, mm(one_hot(hits), feat[pl.ds(pl.multiple_of(g * PGRP, PGRP), PGRP), :])))
        for aligned, rows in todo:
            append(packed, rows, aligned)

    wait_quarter(0)
    stencil(0)
    wait_quarter(1)
    scal_copy.wait()

    def both_steps(i, carry):
        @pl.when((lax.rem(i, 2) == 1) & (i > 1))
        def _():
            wait_quarter(lax.div(i, 2) + 1)

        stencil(i)
        pack(i - 1)
        return carry

    lax.fori_loop(1, 7, both_steps, 0)
    stencil(7)
    pack(6)
    pack(7)
    lon_lo[...] = st[LAT : 2 * LAT, :]
    lon_hi[...] = st[COLS : COLS + LAT, :]
    lat_lo[...] = st[pl.ds(LAT, LON, stride=LAT), :]
    lat_hi[...] = st[pl.ds(2 * LAT - 1, LON, stride=LAT), :]
    for c in w_copies:
        c.wait()

    before, _, _ = plan(scal)
    weights, hidden = (w_in, w_hid, w_out), (ha, hb)

    closure_units(packed, tend, weights, hidden, 0, before)


def closure_units(packed, tend, weights, hidden, first, end):
    def rows(unit, size):
        part = pl.ds(pl.multiple_of(unit * UNIT, UNIT), size)
        tend[part, :] = closure_tile(packed[part, :], *weights, *hidden)

    odd = lax.rem(end - first, 2)

    @pl.when(odd == 1)
    def _():
        rows(first, UNIT)

    def tile(t, carry):
        rows(first + odd + 2 * t, TILE)
        return carry

    lax.fori_loop(0, lax.div(end - first, 2), tile, 0)


def plan(scal):
    inner_n = scal[0, LON - 1]
    count = inner_n + scal[1, 0]
    total = lax.div(count + UNIT - 1, UNIT)
    place = lax.axis_index("ty")
    more = jnp.where(place <= 1, 2, jnp.where(place <= 3, 1, 0))
    inner = lax.div(inner_n, UNIT)
    before = jnp.minimum(jnp.clip(lax.div(count, UNIT) - 4 + more, 0, EARLY_UNITS - 2 + more), inner)
    less = (inner > before) & (lax.rem(inner - before, 2) == 1) & (total - inner < 2)
    return before, jnp.where(less, inner - 1, inner), total


def middle_kernel(packed, tend_f, scal, w_in, w_hid, w_out, tend, ha, hb):
    early = EARLY_UNITS * UNIT
    tend[:early, :] = tend_f[...]
    tend[early:, :] = jnp.zeros((ROWS - early, CH), BF)
    before, inner, _ = plan(scal)
    closure_units(packed, tend, (w_in, w_hid, w_out), (ha, hb), before, inner)


def last_kernel(
    west, east, south, north, adv_i, packed_i, tend_i, rank_t, rank_e, scal, coef, w_in, w_hid, w_out,
    out_h, adv, packed, tend, ha, hb, sem,
):
    adv[0:LAT, :] += west[...] * coef[2 * LON : 2 * LON + LAT, :]
    adv[COLS - LAT :, :] += east[...] * coef[2 * LON + LAT :, :]
    low, high = pl.ds(0, LON, stride=LAT), pl.ds(LAT - 1, LON, stride=LAT)
    place = lax.axis_index("ty")
    north_rim = jnp.where(place == lax.axis_size("ty") - 1, F32(0.0), north[...])
    south_rim = jnp.where(place == 0, F32(0.0), south[...])
    adv[high, :] = adv[high, :] + north_rim * coef[:LON, :]
    adv[low, :] = adv[low, :] + south_rim * coef[LON : 2 * LON, :]
    edge = jnp.concatenate(
        [adv[0:LAT, :], adv[COLS - LAT :, :], jnp.zeros((64, CH), F32), adv[low, :], adv[high, :]], axis=0
    ).astype(BF)
    inner_n = scal[0, LON - 1]
    aligned_e = align16(inner_n)
    hits = iota((320 + 16, EDGE), 0) == rank_e[:1, :] - aligned_e
    append(packed, mm(one_hot(hits), edge), aligned_e)

    def unpacked(q):
        turned = pltpu.roll(rank_t[...], lax.rem(LON - q * 16, LON), 1)
        parts = []
        for i in range(4):
            aligned = align16(scal[0, q * 16 + 4 * i])
            cols = [jnp.broadcast_to(turned[:, 4 * i + j : 4 * i + j + 1], (LAT, 256)) for j in range(4)]
            hit = one_hot(jnp.concatenate(cols, axis=0) == iota((UGRP, 256), 1) + aligned)
            parts.append(mm(hit, tend[pl.ds(aligned, 256), :]))
        r = pl.multiple_of(q * 4 * UGRP, 4 * UGRP)
        adv[pl.ds(r, 4 * UGRP), :] += jnp.concatenate(parts, axis=0)

    _, done, total = plan(scal)
    ready = scal[0, EARLY * 16]
    early_tile = (total - done >= 2) & (ready <= (total - 2) * UNIT)
    early_unit = (total - done == 1) & (ready <= (total - 1) * UNIT)
    early = early_tile | early_unit
    weights, hidden = (w_in, w_hid, w_out), (ha, hb)
    plain = jnp.where(early_tile, total - 2, jnp.where(early_unit, total - 1, total))
    closure_units(packed, tend, weights, hidden, done, plain)

    def last_rows(first, size):
        part = pl.ds(pl.multiple_of(first * UNIT, UNIT), size)
        beside = [functools.partial(unpacked, q) for q in range(EARLY)]
        tend[part, :] = closure_tile(packed[part, :], *weights, *hidden, beside)

    @pl.when(early_tile)
    def _():
        last_rows(total - 2, TILE)

    @pl.when(early_unit)
    def _():
        last_rows(total - 1, UNIT)

    rank_col = jnp.concatenate(
        [jnp.transpose(jnp.broadcast_to(rank_e[:1, k * 128 : k * 128 + 128], (128, 128))) for k in range(3)], axis=0
    )
    picks = jnp.concatenate([rank_col - aligned_e - 128 * k for k in range(3)], axis=1) == (
        iota((EDGE, EDGE), 1) & 127
    )
    back = mm(one_hot(picks), tend[pl.ds(aligned_e, EDGE), :])
    adv[0:LAT, :] += back[0:LAT]
    adv[COLS - LAT :, :] += back[LAT : 2 * LAT]
    adv[low, :] = adv[low, :] + back[128:256]
    adv[high, :] = adv[high, :] + back[256:384]

    def out_copy(k):
        part = pl.ds(k * (COLS // 8), COLS // 8)
        return pltpu.make_async_copy(adv.at[part], out_h.at[part], sem.at[k])

    def unpack(q, carry):
        @pl.when(jnp.logical_not(early) | (q >= EARLY))
        def _():
            unpacked(q)

        out_copy(q).start()
        return carry

    lax.fori_loop(0, 8, unpack, 0)
    for k in range(8):
        out_copy(k).wait()


ANY = pl.BlockSpec(memory_space=pl.ANY)
HBM = pl.BlockSpec(memory_space=pltpu.HBM)
VM = pl.BlockSpec(memory_space=pltpu.VMEM)
SM = pl.BlockSpec(memory_space=pltpu.SMEM)


def in_hbm(x):
    return pltpu.with_memory_space_constraint(x, pltpu.HBM)


def params():
    return pltpu.CompilerParams(vmem_limit_bytes=24 << 20)


def cost(gflops):
    return pl.CostEstimate(flops=gflops * 10**9, bytes_accessed=1 << 20, transcendentals=1 << 20)


def local(state, courant, diffusion, conv_mask, w_in, w_hidden, w_out):
    n_tx, n_ty = lax.axis_size("tx"), lax.axis_size("ty")
    ring = [(i, (i + 1) % n_tx) for i in range(n_tx)]
    line = [(i, (i + 1) % n_ty) for i in range(n_ty)]
    kept = (
        ((COLS, CH), F32),
        ((ROWS, CH), BF),
        ((EARLY_UNITS * UNIT, CH), BF),
        ((LAT, LON), I32),
        ((8, EDGE), I32),
        None,
        ((2 * LON + 2 * LAT, CH), F32),
        ((CH, HID), BF),
        ((3, HID, HID), BF),
        ((HID, CH), BF),
        ((LAT, CH), F32),
        ((LAT, CH), F32),
        ((LON, CH), F32),
        ((LON, CH), F32),
    )
    hidden = [pltpu.VMEM((TILE, HID), BF)] * 2
    held = pl.pallas_call(
        first_kernel,
        out_shape=[pltpu.VMEM(*k) if k else pltpu.SMEM((8, LON), I32) for k in kept],
        in_specs=[HBM] * 7,
        out_specs=[VM if k else SM for k in kept],
        scratch_shapes=[
            pltpu.VMEM((COLS + 2 * LAT + 8, CH), F32),
            pltpu.VMEM((COLS, CH), BF),
            pltpu.VMEM((COLS, CH), BF),
            pltpu.VMEM((LAT, LON), F32),
            pltpu.VMEM((LON, LON), F32),
            pltpu.VMEM((LAT, LON), I32),
            pltpu.VMEM((LON, LON), F32),
            pltpu.VMEM((COLS // PGRP, PGRP), I32),
            *hidden,
            pltpu.VMEM((8, LON), I32),
            pltpu.SemaphoreType.DMA((13,)),
            pltpu.SemaphoreType.DMA,
        ],
        compiler_params=params(),
        cost_estimate=cost(1),
        name="advance_pack",
    )(*map(in_hbm, (state.reshape(COLS, CH), courant.reshape(COLS, CH), diffusion.T, conv_mask.T, w_in, w_hidden, w_out)))
    adv, packed, tend_f, rank_t, rank_e, scal, coef, w_in, w_hid, w_out, lon_lo, lon_hi, lat_lo, lat_hi = held
    west = lax.ppermute(lon_hi, "tx", ring)
    east = lax.ppermute(lon_lo, "tx", [(j, i) for i, j in ring])
    south = lax.ppermute(lat_hi, "ty", line)
    north = lax.ppermute(lat_lo, "ty", [(j, i) for i, j in line])
    tend = pl.pallas_call(
        middle_kernel,
        out_shape=pltpu.VMEM((ROWS, CH), BF),
        in_specs=[VM, VM, SM, VM, VM, VM],
        out_specs=VM,
        scratch_shapes=hidden,
        compiler_params=params(),
        cost_estimate=cost(12),
        name="closure_middle",
    )(packed, tend_f, scal, w_in, w_hid, w_out)
    out, *_ = pl.pallas_call(
        last_kernel,
        out_shape=[
            jax.ShapeDtypeStruct((COLS, CH), F32),
            pltpu.VMEM((COLS, CH), F32),
            pltpu.VMEM((ROWS, CH), BF),
            pltpu.VMEM((ROWS, CH), BF),
        ],
        in_specs=[VM] * 9 + [SM] + [VM] * 4,
        out_specs=[HBM, VM, VM, VM],
        input_output_aliases={4: 1, 5: 2, 6: 3},
        scratch_shapes=[*hidden, pltpu.SemaphoreType.DMA((8,))],
        compiler_params=params(),
        cost_estimate=cost(4),
        name="closure_unpack",
    )(west, east, south, north, adv, packed, tend, rank_t, rank_e, scal, coef, w_in, w_hid, w_out)
    return out.reshape(LON, LAT, CH)


def solution(mesh):
    tile = P(("member", "tx"), "ty", None)
    flat = P(("member", "tx"), "ty")
    return jax.shard_map(
        local,
        mesh=mesh,
        in_specs=(tile, tile, flat, flat, P(), P(), P()),
        out_specs=tile,
        check_vma=False,
    )
```

```python
import functools

import jax
import jax.numpy as jnp
from jax import lax
from jax.experimental import pallas as pl
from jax.experimental.pallas import tpu as pltpu
from jax.sharding import PartitionSpec as P

LON, LAT, CH, HID = 128, 32, 128, 1024
COLS = LON * LAT
TILE = 512
CAP = 2048
ROWS = CAP + TILE
PGRP = 128
UGRP = 128
EDGE = 384
EARLY = 6
UNIT = 256
EARLY_UNITS = 4
BF, F32, I32 = jnp.bfloat16, jnp.float32, jnp.int32


def iota(shape, dim):
    return lax.broadcasted_iota(I32, shape, dim)


def one_hot(hit):
    return jnp.where(hit, F32(1.0), F32(0.0)).astype(BF)


def mm(a, b):
    return jnp.dot(a, b, preferred_element_type=F32)


def silu(v):
    half = 0.5 * v
    return (half + half * jnp.tanh(half)).astype(BF)


def closure_tile(x, w_in, w_hid, w_out, ha, hb, beside=()):
    step = 256
    beside = list(beside)
    ha, hb = ha.at[: x.shape[0]], hb.at[: x.shape[0]]

    def layer(src, weight, dst, side):
        for n in range(0, HID, step):
            dst[:, n : n + step] = silu(mm(src, weight(n)))
            if side and n in (0, 512) and beside:
                beside.pop(0)()

    layer(x, lambda n: w_in[:, n : n + step], ha, True)
    layer(ha[...], lambda n: w_hid[0, :, n : n + step], hb, True)
    layer(hb[...], lambda n: w_hid[1, :, n : n + step], ha, True)
    layer(ha[...], lambda n: w_hid[2, :, n : n + step], hb, True)
    return mm(hb[...], w_out[...]).astype(BF)


def append(packed, rows, aligned):
    n = rows.shape[0]
    head = packed[pl.ds(aligned, 16), :].astype(F32) + rows[:16]
    packed[pl.ds(aligned, 16), :] = head.astype(BF)
    packed[pl.ds(pl.multiple_of(aligned + 16, 16), n - 16), :] = rows[16:].astype(BF)


def align16(x):
    return pl.multiple_of((x // 16) * 16, 16)


def first_kernel(
    state_h, courant_h, diff_h, mask_h, win_h, whid_h, wout_h,
    adv, packed, tend, rank_t, rank_e, scal, coef, w_in, w_hid, w_out, lon_lo, lon_hi, lat_lo, lat_hi,
    st, cou, feat, dif, dif_n, msk, rank_n, rank_r, ha, hb, scal_v, sem, sem_s,
):
    quarter = COLS // 4

    def in_copies(k):
        return (
            pltpu.make_async_copy(state_h.at[pl.ds(k * quarter, quarter)], st.at[pl.ds(k * quarter + LAT, quarter)], sem.at[k]),
            pltpu.make_async_copy(courant_h.at[pl.ds(k * quarter, quarter)], cou.at[pl.ds(k * quarter, quarter)], sem.at[4 + k]),
        )

    mask_copy = pltpu.make_async_copy(mask_h, msk, sem.at[8])
    diff_copy = pltpu.make_async_copy(diff_h, dif, sem.at[9])
    w_copies = (
        pltpu.make_async_copy(win_h, w_in, sem.at[10]),
        pltpu.make_async_copy(whid_h, w_hid, sem.at[11]),
        pltpu.make_async_copy(wout_h, w_out, sem.at[12]),
    )
    mask_copy.start()
    diff_copy.start()
    for k in range(4):
        for c in in_copies(k):
            c.start()
    for c in w_copies:
        c.start()
    packed[...] = jnp.zeros_like(packed)
    tend[...] = jnp.zeros_like(tend)
    st[0:LAT, :] = jnp.zeros((LAT, CH), F32)
    st[COLS + LAT : COLS + 2 * LAT, :] = jnp.zeros((LAT, CH), F32)

    def wait_quarter(k):
        for c in in_copies(k):
            c.wait()

    mask_copy.wait()
    diff_copy.wait()
    dif_1 = dif[...].astype(BF).astype(F32)
    dif_2 = (dif[...] - dif_1).astype(BF).astype(F32)
    dif_3 = dif[...] - dif_1 - dif_2
    dif_n[...] = jnp.transpose(jnp.concatenate([dif_1, dif_2, dif_3, jnp.zeros((LAT, LON), F32)], axis=0))

    lat_of = iota((LAT, CH), 0)
    low = iota((LAT, CH), 1) < 64
    own_lat = (iota((LAT, CH), 1) & 31) == lat_of
    ones = jnp.ones((CH, CH), BF)

    def stencil(i):
        spread = [jnp.where(own_lat, dif_n[pl.ds(i * 16 + j, 1), :], F32(0.0)) for j in range(16)]
        d_all = mm(jnp.concatenate(spread, axis=0).astype(BF), ones)
        for j in range(16):
            r = pl.multiple_of(i * 4 * PGRP + j * LAT, LAT)
            center = st[pl.ds(r + LAT, LAT), :]
            east = st[pl.ds(r + 2 * LAT, LAT), :]
            west = st[pl.ds(r, LAT), :]
            north = jnp.where(lat_of == LAT - 1, F32(0.0), st[pl.ds(r + LAT + 1, LAT), :])
            south = jnp.where(lat_of == 0, F32(0.0), st[pl.ds(r + LAT - 1, LAT), :])
            wind = 0.5 * cou[pl.ds(r, LAT), :].astype(F32)
            turned = pltpu.roll(wind, 64, 1)
            along_lon = jnp.where(low, wind, turned)
            along_lat = jnp.where(low, turned, wind)
            d = d_all[j * LAT : (j + 1) * LAT]
            laplace = east + west + north + south - 4.0 * center
            new = center - along_lon * (east - west) - along_lat * (north - south) + d * laplace
            adv[pl.ds(r, LAT), :] = new
            feat[pl.ds(r, LAT), :] = new.astype(BF)
            coef[pl.ds(i * 16 + j, 1), :] = (d - along_lat)[LAT - 1 :]
            coef[pl.ds(LON + i * 16 + j, 1), :] = (d + along_lat)[:1]
            if isinstance(i, int) and i == 0 and j == 0:
                coef[2 * LON : 2 * LON + LAT, :] = d + along_lon
            if isinstance(i, int) and i == 7 and j == 15:
                coef[2 * LON + LAT : 2 * LON + 2 * LAT, :] = d - along_lon

    lat, lon = iota((LAT, LON), 0), iota((LAT, LON), 1)
    flags = msk[...]
    inner = (lon > 0) & (lon < LON - 1) & (lat > 0) & (lat < LAT - 1) & (flags == 1)
    inner_b = one_hot(inner)
    in_row = mm(one_hot(iota((LAT, LAT), 1) < iota((LAT, LAT), 0)), inner_b)
    per_lon = mm(jnp.ones((LAT, LAT), BF), inner_b).astype(BF)
    row_start = mm(per_lon, one_hot(iota((LON, LON), 0) < iota((LON, LON), 1)))
    rank = jnp.where(inner, in_row + row_start, F32(-4096.0))
    rank_t[...] = rank.astype(I32)
    starts = row_start[:1]
    flags_f = flags.astype(F32)
    lane = iota((1, LON), 1)
    ends = (lane == 0) | (lane == LON - 1)
    both = jnp.concatenate([rank, flags_f, jnp.zeros((LON - 2 * LAT, LON), F32)], axis=0)
    rank_n[...] = jnp.transpose(both)
    edge_row = jnp.concatenate(
        [
            rank_n[0:1, LAT : 2 * LAT],
            rank_n[LON - 1 :, LAT : 2 * LAT],
            jnp.zeros((1, 64), F32),
            jnp.where(ends, F32(0.0), flags_f[:1]),
            jnp.where(ends, F32(0.0), flags_f[LAT - 1 :]),
        ],
        axis=1,
    )
    edge_n = jnp.broadcast_to(jnp.sum(edge_row, axis=1, keepdims=True), (1, LON))
    scal_v[...] = jnp.where(iota((8, LON), 0) == 0, starts, edge_n).astype(I32)
    scal_copy = pltpu.make_async_copy(scal_v, scal, sem_s)
    scal_copy.start()
    rank_r[...] = jnp.concatenate(
        [rank_n[pl.ds(j, COLS // PGRP, stride=PGRP // LAT), :LAT] for j in range(PGRP // LAT)], axis=1
    ).astype(I32)
    edge_b = jnp.broadcast_to(edge_row, (16, EDGE)).astype(BF)
    edge_rank = mm(edge_b, one_hot(iota((EDGE, EDGE), 0) < iota((EDGE, EDGE), 1)))[:8]
    rank_e[...] = jnp.where(edge_row == 1.0, edge_rank + starts[:, LON - 1 :], F32(-4096.0)).astype(I32)
    def pack(i):
        todo = []
        for k in range(4):
            g = i * 4 + k
            aligned = align16(scal[0, g * 4])
            hits = iota((PGRP + 16, PGRP), 0) == rank_r[pl.ds(g, 1), :] - aligned
            todo.append((aligned, mm(one_hot(hits), feat[pl.ds(pl.multiple_of(g * PGRP, PGRP), PGRP), :])))
        for aligned, rows in todo:
            append(packed, rows, aligned)

    wait_quarter(0)
    stencil(0)
    wait_quarter(1)
    scal_copy.wait()

    def both_steps(i, carry):
        @pl.when((lax.rem(i, 2) == 1) & (i > 1))
        def _():
            wait_quarter(lax.div(i, 2) + 1)

        stencil(i)
        pack(i - 1)
        return carry

    lax.fori_loop(1, 7, both_steps, 0)
    stencil(7)
    pack(6)
    pack(7)
    lon_lo[...] = st[LAT : 2 * LAT, :]
    lon_hi[...] = st[COLS : COLS + LAT, :]
    lat_lo[...] = st[pl.ds(LAT, LON, stride=LAT), :]
    lat_hi[...] = st[pl.ds(2 * LAT - 1, LON, stride=LAT), :]
    for c in w_copies:
        c.wait()

    before, _, _ = plan(scal)
    weights, hidden = (w_in, w_hid, w_out), (ha, hb)

    closure_units(packed, tend, weights, hidden, 0, before)


def closure_units(packed, tend, weights, hidden, first, end):
    def rows(unit, size):
        part = pl.ds(pl.multiple_of(unit * UNIT, UNIT), size)
        tend[part, :] = closure_tile(packed[part, :], *weights, *hidden)

    odd = lax.rem(end - first, 2)

    @pl.when(odd == 1)
    def _():
        rows(first, UNIT)

    def tile(t, carry):
        rows(first + odd + 2 * t, TILE)
        return carry

    lax.fori_loop(0, lax.div(end - first, 2), tile, 0)


def plan(scal):
    inner_n = scal[0, LON - 1]
    count = inner_n + scal[1, 0]
    total = lax.div(count + UNIT - 1, UNIT)
    place = lax.axis_index("ty")
    more = jnp.where(place <= 1, 2, jnp.where(place <= 3, 1, 0))
    inner = lax.div(inner_n, UNIT)
    before = jnp.minimum(jnp.clip(lax.div(count, UNIT) - 4 + more, 0, EARLY_UNITS - 2 + more), inner)
    less = (inner > before) & (lax.rem(inner - before, 2) == 1) & (total - inner < 2)
    return before, jnp.where(less, inner - 1, inner), total


def middle_kernel(packed, tend_f, scal, w_in, w_hid, w_out, tend, ha, hb):
    early = EARLY_UNITS * UNIT
    tend[:early, :] = tend_f[...]
    tend[early:, :] = jnp.zeros((ROWS - early, CH), BF)
    before, inner, _ = plan(scal)
    closure_units(packed, tend, (w_in, w_hid, w_out), (ha, hb), before, inner)


def last_kernel(
    west, east, south, north, adv_i, packed_i, tend_i, rank_t, rank_e, scal, coef, w_in, w_hid, w_out,
    out_h, adv, packed, tend, ha, hb, edge_hot, sem,
):
    adv[0:LAT, :] += west[...] * coef[2 * LON : 2 * LON + LAT, :]
    adv[COLS - LAT :, :] += east[...] * coef[2 * LON + LAT :, :]
    low, high = pl.ds(0, LON, stride=LAT), pl.ds(LAT - 1, LON, stride=LAT)
    place = lax.axis_index("ty")
    north_rim = jnp.where(place == lax.axis_size("ty") - 1, F32(0.0), north[...])
    south_rim = jnp.where(place == 0, F32(0.0), south[...])
    adv[high, :] = adv[high, :] + north_rim * coef[:LON, :]
    adv[low, :] = adv[low, :] + south_rim * coef[LON : 2 * LON, :]
    edge = jnp.concatenate(
        [adv[0:LAT, :], adv[COLS - LAT :, :], jnp.zeros((64, CH), F32), adv[low, :], adv[high, :]], axis=0
    ).astype(BF)
    inner_n = scal[0, LON - 1]
    aligned_e = align16(inner_n)
    hits = iota((320 + 16, EDGE), 0) == rank_e[:1, :] - aligned_e
    append(packed, mm(one_hot(hits), edge), aligned_e)

    def unpacked(q):
        turned = pltpu.roll(rank_t[...], lax.rem(LON - q * 16, LON), 1)
        parts = []
        for i in range(4):
            aligned = align16(scal[0, q * 16 + 4 * i])
            cols = [jnp.broadcast_to(turned[:, 4 * i + j : 4 * i + j + 1], (LAT, 256)) for j in range(4)]
            hit = one_hot(jnp.concatenate(cols, axis=0) == iota((UGRP, 256), 1) + aligned)
            parts.append(mm(hit, tend[pl.ds(aligned, 256), :]))
        r = pl.multiple_of(q * 4 * UGRP, 4 * UGRP)
        adv[pl.ds(r, 4 * UGRP), :] += jnp.concatenate(parts, axis=0)

    _, done, total = plan(scal)
    def edge_picks():
        rank_col = jnp.concatenate(
            [jnp.transpose(jnp.broadcast_to(rank_e[:1, k * 128 : k * 128 + 128], (128, 128))) for k in range(3)], axis=0
        )
        picks = jnp.concatenate([rank_col - aligned_e - 128 * k for k in range(3)], axis=1) == (
            iota((EDGE, EDGE), 1) & 127
        )
        edge_hot[...] = one_hot(picks)

    ready = scal[0, EARLY * 16]
    early_tile = (total - done >= 2) & (ready <= (total - 2) * UNIT)
    early_unit = (total - done == 1) & (ready <= (total - 1) * UNIT)
    early = early_tile | early_unit
    weights, hidden = (w_in, w_hid, w_out), (ha, hb)
    plain = jnp.where(early_tile, total - 2, jnp.where(early_unit, total - 1, total))
    closure_units(packed, tend, weights, hidden, done, plain)

    def last_rows(first, size):
        part = pl.ds(pl.multiple_of(first * UNIT, UNIT), size)
        beside = [edge_picks] + [functools.partial(unpacked, q) for q in range(EARLY)]
        tend[part, :] = closure_tile(packed[part, :], *weights, *hidden, beside)

    @pl.when(jnp.logical_not(early))
    def _():
        edge_picks()

    @pl.when(early_tile)
    def _():
        last_rows(total - 2, TILE)

    @pl.when(early_unit)
    def _():
        last_rows(total - 1, UNIT)

    back = mm(edge_hot[...], tend[pl.ds(aligned_e, EDGE), :])
    adv[0:LAT, :] += back[0:LAT]
    adv[COLS - LAT :, :] += back[LAT : 2 * LAT]
    adv[low, :] = adv[low, :] + back[128:256]
    adv[high, :] = adv[high, :] + back[256:384]

    def out_copy(k):
        part = pl.ds(k * (COLS // 8), COLS // 8)
        return pltpu.make_async_copy(adv.at[part], out_h.at[part], sem.at[k])

    def unpack(q, carry):
        @pl.when(jnp.logical_not(early) | (q >= EARLY))
        def _():
            unpacked(q)

        out_copy(q).start()
        return carry

    lax.fori_loop(0, 8, unpack, 0)
    for k in range(8):
        out_copy(k).wait()


ANY = pl.BlockSpec(memory_space=pl.ANY)
HBM = pl.BlockSpec(memory_space=pltpu.HBM)
VM = pl.BlockSpec(memory_space=pltpu.VMEM)
SM = pl.BlockSpec(memory_space=pltpu.SMEM)


def in_hbm(x):
    return pltpu.with_memory_space_constraint(x, pltpu.HBM)


def params():
    return pltpu.CompilerParams(vmem_limit_bytes=24 << 20)


def cost(gflops):
    return pl.CostEstimate(flops=gflops * 10**9, bytes_accessed=1 << 20, transcendentals=1 << 20)


def local(state, courant, diffusion, conv_mask, w_in, w_hidden, w_out):
    n_tx, n_ty = lax.axis_size("tx"), lax.axis_size("ty")
    ring = [(i, (i + 1) % n_tx) for i in range(n_tx)]
    line = [(i, (i + 1) % n_ty) for i in range(n_ty)]
    kept = (
        ((COLS, CH), F32),
        ((ROWS, CH), BF),
        ((EARLY_UNITS * UNIT, CH), BF),
        ((LAT, LON), I32),
        ((8, EDGE), I32),
        None,
        ((2 * LON + 2 * LAT, CH), F32),
        ((CH, HID), BF),
        ((3, HID, HID), BF),
        ((HID, CH), BF),
        ((LAT, CH), F32),
        ((LAT, CH), F32),
        ((LON, CH), F32),
        ((LON, CH), F32),
    )
    hidden = [pltpu.VMEM((TILE, HID), BF)] * 2
    held = pl.pallas_call(
        first_kernel,
        out_shape=[pltpu.VMEM(*k) if k else pltpu.SMEM((8, LON), I32) for k in kept],
        in_specs=[HBM] * 7,
        out_specs=[VM if k else SM for k in kept],
        scratch_shapes=[
            pltpu.VMEM((COLS + 2 * LAT + 8, CH), F32),
            pltpu.VMEM((COLS, CH), BF),
            pltpu.VMEM((COLS, CH), BF),
            pltpu.VMEM((LAT, LON), F32),
            pltpu.VMEM((LON, LON), F32),
            pltpu.VMEM((LAT, LON), I32),
            pltpu.VMEM((LON, LON), F32),
            pltpu.VMEM((COLS // PGRP, PGRP), I32),
            *hidden,
            pltpu.VMEM((8, LON), I32),
            pltpu.SemaphoreType.DMA((13,)),
            pltpu.SemaphoreType.DMA,
        ],
        compiler_params=params(),
        cost_estimate=cost(1),
        name="advance_pack",
    )(*map(in_hbm, (state.reshape(COLS, CH), courant.reshape(COLS, CH), diffusion.T, conv_mask.T, w_in, w_hidden, w_out)))
    adv, packed, tend_f, rank_t, rank_e, scal, coef, w_in, w_hid, w_out, lon_lo, lon_hi, lat_lo, lat_hi = held
    west = lax.ppermute(lon_hi, "tx", ring)
    east = lax.ppermute(lon_lo, "tx", [(j, i) for i, j in ring])
    south = lax.ppermute(lat_hi, "ty", line)
    north = lax.ppermute(lat_lo, "ty", [(j, i) for i, j in line])
    tend = pl.pallas_call(
        middle_kernel,
        out_shape=pltpu.VMEM((ROWS, CH), BF),
        in_specs=[VM, VM, SM, VM, VM, VM],
        out_specs=VM,
        scratch_shapes=hidden,
        compiler_params=params(),
        cost_estimate=cost(12),
        name="closure_middle",
    )(packed, tend_f, scal, w_in, w_hid, w_out)
    out, *_ = pl.pallas_call(
        last_kernel,
        out_shape=[
            jax.ShapeDtypeStruct((COLS, CH), F32),
            pltpu.VMEM((COLS, CH), F32),
            pltpu.VMEM((ROWS, CH), BF),
            pltpu.VMEM((ROWS, CH), BF),
        ],
        in_specs=[VM] * 9 + [SM] + [VM] * 4,
        out_specs=[HBM, VM, VM, VM],
        input_output_aliases={4: 1, 5: 2, 6: 3},
        scratch_shapes=[*hidden, pltpu.VMEM((EDGE, EDGE), BF), pltpu.SemaphoreType.DMA((8,))],
        compiler_params=params(),
        cost_estimate=cost(4),
        name="closure_unpack",
    )(west, east, south, north, adv, packed, tend, rank_t, rank_e, scal, coef, w_in, w_hid, w_out)
    return out.reshape(LON, LAT, CH)


def solution(mesh):
    tile = P(("member", "tx"), "ty", None)
    flat = P(("member", "tx"), "ty")
    return jax.shard_map(
        local,
        mesh=mesh,
        in_specs=(tile, tile, flat, flat, P(), P(), P()),
        out_specs=tile,
        check_vma=False,
    )
```
